32 devices in a mesh: section: 2 (over y), head: 4 (over x, core), blk: 4 (over z).
Axes of the slice: x: 2, y: 2, z: 4, core: 2. Of those that a mesh axis runs over, the one named last changes fastest.
Arguments:
- tokens: bfloat16 [4, 1792, 768], P(None, ('head', 'blk')), may hold values from -6 to 6
- cotangent: float32 [4, 1792, 768], P(None, ('head', 'blk')), may hold values from -6 to 6
- doc_ids: int32 [4, 1792], P(None, ('head', 'blk')), may hold values from 0 to 10, as said below
- pad_mask: int32 [4, 1792], P(None, ('head', 'blk')), may hold values from 0 to 1, as said below
- w_query: bfloat16 [2, 768, 768], P('section', ('head', 'blk')), may hold values from -0.21875 to 0.21875
- w_key: bfloat16 [2, 768, 768], P('section', ('head', 'blk')), may hold values from -0.21875 to 0.21875
- w_value: bfloat16 [2, 768, 768], P('section', ('head', 'blk')), may hold values from -0.21875 to 0.21875
- w_out: bfloat16 [2, 768, 768], P('section', ('head', 'blk')), may hold values from -0.875 to 0.875
- b_query: bfloat16 [2, 768], P('section', ('head', 'blk')), may hold values from -1.5 to 1.5
- b_value: bfloat16 [2, 768], P('section', ('head', 'blk')), may hold values from -1.5 to 1.5
- b_out: bfloat16 [2, 768], P('section', ('head', 'blk')), may hold values from -1.5 to 1.5
- gain_attn: bfloat16 [2, 768], P('section', ('head', 'blk')), may hold values from 0.5 to 1.5
- bias_attn: bfloat16 [2, 768], P('section', ('head', 'blk')), may hold values from -1.5 to 1.5
- w_up: bfloat16 [2, 768, 3072], P('section', ('head', 'blk')), may hold values from -0.21875 to 0.21875
- b_up: bfloat16 [2, 3072], P('section', ('head', 'blk')), may hold values from -1.5 to 1.5
- w_down: bfloat16 [2, 3072, 768], P('section', ('head', 'blk')), may hold values from -0.109375 to 0.109375
- b_down: bfloat16 [2, 768], P('section', ('head', 'blk')), may hold values from -1.5 to 1.5
- gain_ffn: bfloat16 [2, 768], P('section', ('head', 'blk')), may hold values from 0.5 to 1.5
- bias_ffn: bfloat16 [2, 768], P('section', ('head', 'blk')), may hold values from -1.5 to 1.5
Outputs:
- layer_outputs: bfloat16 [2, 4, 1792, 768], P('section', None, ('head', 'blk'))
- input_grads: float32 [2, 4, 1792, 768], P('section', None, ('head', 'blk'))
- grad_w_query: float32 [2, 768, 768], P('section', ('head', 'blk'))
- grad_w_key: float32 [2, 768, 768], P('section', ('head', 'blk'))
- grad_w_value: float32 [2, 768, 768], P('section', ('head', 'blk'))
- grad_w_out: float32 [2, 768, 768], P('section', ('head', 'blk'))
- grad_b_query: float32 [2, 768], P('section', ('head', 'blk'))
- grad_b_value: float32 [2, 768], P('section', ('head', 'blk'))
- grad_b_out: float32 [2, 768], P('section', ('head', 'blk'))
- grad_gain_attn: float32 [2, 768], P('section', ('head', 'blk'))
- grad_bias_attn: float32 [2, 768], P('section', ('head', 'blk'))
- grad_w_up: float32 [2, 768, 3072], P('section', ('head', 'blk'))
- grad_b_up: float32 [2, 3072], P('section', ('head', 'blk'))
- grad_w_down: float32 [2, 3072, 768], P('section', ('head', 'blk'))
- grad_b_down: float32 [2, 768], P('section', ('head', 'blk'))
- grad_gain_ffn: float32 [2, 768], P('section', ('head', 'blk'))
- grad_bias_ffn: float32 [2, 768], P('section', ('head', 'blk'))
The draws below stay inside these ranges and needn't reach their ends.
Inputs may be any that keep to these rules, and one draw needn't show every extreme that they name: `doc_ids`: document number of each token within its micro-batch: 0 at the first token, rising by one at the first token of each document and never falling; the padding belongs to the last document. Each micro-batch holds exactly 11 documents. `pad_mask`: 0 exactly on the last 1 to 223 tokens of each micro-batch (padding), 1 elsewhere; the last document holds at least one real token.
All inputs are finite; a program needn't handle non-finite values.
Results may differ from the reference program's by a relative error of at most 0.03.
Values may be sent and summed in bfloat16 or wider, within the bound.
No kernel may reach another device: no remote copies, remote signals or barrier semaphores. Data moves between devices by JAX's collectives and lax.ppermute only.
A program may use at most 320 MiB of HBM per device.

```python
from functools import partial
import jax
import jax.numpy as jnp
from jax import lax

D = 768
HEADS = 12
HEAD_DIM = 64
FF = 3072
MICRO = 4
TOK_DEV = 112
TOKENS = 1792
QUARTER = 448
N_SECTION = 2
N_HEAD = 4
N_BLK = 4


def packing(key):

    def single(subkey):
        streams = jax.random.split(subkey, 5)
        places = jnp.arange(TOKENS, dtype=jnp.int32)
        chosen = jax.random.randint(streams[1], (), 0, N_HEAD - 1)
        front = jax.random.randint(streams[2], (), 1, TOK_DEV)
        ending = jax.random.randint(streams[3], (), 2, TOK_DEV)
        opening = chosen * QUARTER + front
        finish = chosen * QUARTER + QUARTER - ending + 1
        padding = jax.random.randint(streams[4], (), 1, 2 * TOK_DEV)
        padded = places >= TOKENS - padding
        eligible = (places > 0) & ((places < opening) | (places > finish)) & jnp.logical_not(padded)
        scores = jax.random.randint(streams[0], (TOKENS,), 0, TOKENS) * TOKENS + places
        scores = jnp.where(eligible, scores, -1)
        unused, picked = lax_top(scores)
        flags = jnp.zeros((TOKENS,), jnp.int32).at[picked].set(1)
        flags = jnp.where((places == opening) | (places == finish) | (places == 0), 1, flags)
        numbers = jnp.cumsum(flags).astype(jnp.int32) - 1
        return (numbers, 1 - padded.astype(jnp.int32))
    return jax.vmap(single)(jax.random.split(key, MICRO))


def lax_top(scores):
    return jax.lax.top_k(scores, TOKENS // (2 * TOK_DEV))


def draw_doc_ids(key, part):
    numbers, marks = packing(key)
    return numbers


def draw_pad_mask(key, part):
    numbers, marks = packing(key)
    return marks


def shard_levels(key, extent, cuts, low, high):
    level, own = 1.0, jax.random.fold_in(key, 6)
    for axis_at, parts in cuts:
        heights = jnp.exp(jax.random.uniform(jax.random.fold_in(own, axis_at), (parts,), jnp.float32, low / len(cuts), high / len(cuts)))
        level = level * jnp.repeat(heights, extent[axis_at] // parts).reshape([-1 if axis == axis_at else 1 for axis in range(len(extent))])
    return level


def normal_values(stream_key, dims, deviation, reach, shards=(), held_as=jnp.bfloat16):
    values = jax.random.normal(stream_key, dims, jnp.float32) * deviation
    if len(shards) > 0:
        values = shard_levels(stream_key, dims, shards, -0.22, 0.18) * values
    return jnp.clip(values, min=-reach, max=reach).astype(held_as)


def setup_inputs(seed: int = 0) -> dict:
    arg_keys = jax.random.split(jax.random.key(seed), 20)
    tokens = normal_values(arg_keys[0], (MICRO, TOKENS, D), 1.0, 6.0, ((1, 16),))
    cotangent = normal_values(arg_keys[1], (MICRO, TOKENS, D), 1.0, 6.0, ((1, 16),), jnp.float32)
    doc_ids = draw_doc_ids(jax.random.fold_in(arg_keys[19], 71), 0)
    pad_mask = draw_pad_mask(jax.random.fold_in(arg_keys[19], 71), 0)
    w_query = normal_values(arg_keys[4], (N_SECTION, D, D), D ** -0.5, 0.21875, ((0, 2), (1, 16)))
    w_key = normal_values(arg_keys[5], (N_SECTION, D, D), D ** -0.5, 0.21875, ((0, 2), (1, 16)))
    w_value = normal_values(arg_keys[6], (N_SECTION, D, D), D ** -0.5, 0.21875, ((0, 2), (1, 16)))
    w_out = normal_values(arg_keys[7], (N_SECTION, D, D), (D // 16) ** -0.5, 0.875, ((0, 2), (1, 16)))
    b_query = normal_values(arg_keys[8], (N_SECTION, D), 0.3, 1.5, ((0, 2), (1, 16)))
    b_value = normal_values(arg_keys[9], (N_SECTION, D), 0.3, 1.5, ((0, 2), (1, 16)))
    b_out = normal_values(arg_keys[10], (N_SECTION, D), 0.3, 1.5, ((0, 2), (1, 16)))
    gain_attn = jnp.clip(1.0 + 0.1 * jax.random.normal(arg_keys[11], (N_SECTION, D), jnp.float32), 0.5, 1.5).astype(jnp.bfloat16)
    bias_attn = normal_values(arg_keys[12], (N_SECTION, D), 0.3, 1.5, ((0, 2), (1, 16)))
    w_up = normal_values(arg_keys[13], (N_SECTION, D, FF), D ** -0.5, 0.21875, ((0, 2), (1, 16)))
    b_up = normal_values(arg_keys[14], (N_SECTION, FF), 0.3, 1.5, ((0, 2), (1, 16)))
    w_down = normal_values(arg_keys[15], (N_SECTION, FF, D), FF ** -0.5, 0.109375, ((0, 2), (1, 16)))
    b_down = normal_values(arg_keys[16], (N_SECTION, D), 0.3, 1.5, ((0, 2), (1, 16)))
    gain_ffn = jnp.clip(1.0 + 0.1 * jax.random.normal(arg_keys[17], (N_SECTION, D), jnp.float32), 0.5, 1.5).astype(jnp.bfloat16)
    bias_ffn = normal_values(arg_keys[18], (N_SECTION, D), 0.3, 1.5, ((0, 2), (1, 16)))
    return {"tokens": tokens, "cotangent": cotangent, "doc_ids": doc_ids, "pad_mask": pad_mask, "w_query": w_query, "w_key": w_key, "w_value": w_value, "w_out": w_out, "b_query": b_query, "b_value": b_value, "b_out": b_out, "gain_attn": gain_attn, "bias_attn": bias_attn, "w_up": w_up, "b_up": b_up, "w_down": w_down, "b_down": b_down, "gain_ffn": gain_ffn, "bias_ffn": bias_ffn}


exact_mode = lax.Precision.HIGHEST

@jax.custom_vjp
def low(v):
    return lax.optimization_barrier(v.astype(jnp.bfloat16)).astype(jnp.float32)

@jax.custom_vjp
def low_back(v):
    return v

def low_keep(v):
    return (low(v), None)

def low_pass(kept, grad):
    return (grad,)

def back_keep(v):
    return (v, None)

def back_low(kept, grad):
    return (low(grad),)
low.defvjp(low_keep, low_pass)
low_back.defvjp(back_keep, back_low)

def both_ways(value):
    return low_back(low(value))

def matmul(left, right):
    return jnp.dot(left, right, precision=exact_mode, preferred_element_type=jnp.float32)

def layer_norm(value, gain, shift):
    centre = value - lax.optimization_barrier(jnp.mean(value, axis=-1, keepdims=True))
    spread = lax.optimization_barrier(jnp.mean(centre * centre, axis=-1, keepdims=True))
    return centre * lax.rsqrt(spread + 1e-05) * gain + shift

def attend(queries, key_rows, value_rows, query_marks, key_marks):
    row_count = TOKENS // N_BLK

    def one_block(inputs):
        query_block, marks = inputs
        scores = jnp.einsum('qhc,khc->qhk', query_block, key_rows, precision=exact_mode) * 0.125
        scores = low_back(scores)
        allowed = (marks[:, None] == key_marks[None, :])[:, None, :]
        scores = jnp.where(allowed, scores, -1e+30)
        row_max = lax.optimization_barrier(jnp.max(scores, axis=-1, keepdims=True))
        weights = jnp.where(allowed, jnp.exp(scores - row_max), 0.0)
        probabilities = low(weights / lax.optimization_barrier(jnp.sum(weights, axis=-1, keepdims=True)))
        return jnp.einsum('qhk,khc->qhc', probabilities, value_rows, precision=exact_mode)
    attended = lax.map(jax.checkpoint(one_block), (queries.reshape(N_BLK, row_count, HEADS, HEAD_DIM), query_marks.reshape(N_BLK, row_count)))
    return attended.reshape(TOKENS, D)

def layer(layer_in, parameters, query_marks, key_marks):
    q_weight, k_weight, v_weight, o_weight, q_shift, v_shift, o_shift, norm_gain, norm_shift, up_weight, up_shift, down_weight, down_shift, final_gain, final_shift = parameters
    queries = both_ways(matmul(layer_in, q_weight) + q_shift)
    key_rows = both_ways(matmul(layer_in, k_weight))
    value_rows = both_ways(matmul(layer_in, v_weight) + v_shift)
    attended = attend(queries.reshape(TOKENS, HEADS, HEAD_DIM), key_rows.reshape(TOKENS, HEADS, HEAD_DIM), value_rows.reshape(TOKENS, HEADS, HEAD_DIM), query_marks, key_marks)
    attended = both_ways(attended)
    branch = low_back(matmul(attended, o_weight) + o_shift)
    middle = layer_norm(layer_in + branch, norm_gain, norm_shift)
    hidden = low_back(matmul(low(middle), up_weight) + up_shift)
    active = low(jax.nn.gelu(hidden, approximate=False))
    second = low_back(matmul(active, down_weight) + down_shift)
    return layer_norm(middle + second, final_gain, final_shift)

def reference(tokens, cotangent, doc_ids, pad_mask, w_query, w_key, w_value, w_out, b_query, b_value, b_out, gain_attn, bias_attn, w_up, b_up, w_down, b_down, gain_ffn, bias_ffn):
    stacked = tuple((array.astype(jnp.float32) for array in (w_query, w_key, w_value, w_out, b_query, b_value, b_out, gain_attn, bias_attn, w_up, b_up, w_down, b_down, gain_ffn, bias_ffn)))
    totals = [jnp.zeros_like(array) for array in stacked]
    outputs_all = []
    grads_all = []
    for micro_index in range(MICRO):
        query_marks = doc_ids[micro_index]
        key_marks = jnp.where(pad_mask[micro_index] == 1, query_marks, -1)
        current = tokens[micro_index].astype(jnp.float32)
        pullbacks = []
        outputs_micro = []
        for section_index in range(N_SECTION):
            parameters = tuple((array[section_index] for array in stacked))
            result, pullback = jax.vjp(partial(layer, query_marks=query_marks, key_marks=key_marks), current, parameters)
            current = low(result)
            outputs_micro.append(result.astype(jnp.bfloat16))
            pullbacks.append(pullback)
        gradient = cotangent[micro_index].astype(jnp.float32)
        grads_micro = [None] * N_SECTION
        for section_index in reversed(range(N_SECTION)):
            grad_in, grad_params = pullbacks[section_index](gradient)
            grads_micro[section_index] = grad_in
            totals = [total.at[section_index].add(part) for total, part in zip(totals, grad_params)]
            gradient = low(grad_in)
        outputs_all.append(jnp.stack(outputs_micro))
        grads_all.append(jnp.stack(grads_micro))
    layer_outputs = jnp.stack(outputs_all, axis=1)
    input_grads = jnp.stack(grads_all, axis=1)
    return (layer_outputs, input_grads, totals[0], totals[1], totals[2], totals[3], totals[4], totals[5], totals[6], totals[7], totals[8], totals[9], totals[10], totals[11], totals[12], totals[13], totals[14])
```

```python
import functools

import jax
import jax.numpy as jnp
from jax import lax
from jax.experimental import pallas as pl
from jax.experimental.pallas import tpu as pltpu
from jax.sharding import PartitionSpec as P

HEAD_DIM = 64
GROUP = ("head", "blk")
F32 = jnp.float32
BF16 = jnp.bfloat16
NT = (((1,), (1,)), ((), ()))
NN = (((1,), (0,)), ((), ()))
TN = (((0,), (0,)), ((), ()))
VMEM_LIMIT = 48 * 1024 * 1024


def dot(left, right, dims=NN):
    return lax.dot_general(left, right, dims, preferred_element_type=F32)


def head_lanes(value, head):
    lane = lax.broadcasted_iota(jnp.int32, value.shape, 1)
    return jnp.where(lane // HEAD_DIM == head, value, jnp.zeros_like(value))


def attention_forward_kernel(q_ref, kv_ref, qid_ref, mark_ref, out_ref, lse_ref, qm, acc, top, total):
    step = pl.program_id(0)
    heads = qm.shape[0]
    width = q_ref.shape[1]

    @pl.when(step == 0)
    def _():
        scaled = q_ref[...] * jnp.asarray(0.125, BF16)
        for head in range(heads):
            qm[head] = head_lanes(scaled, head)
        acc[...] = jnp.zeros_like(acc)
        top[...] = jnp.full_like(top, -1e30)
        total[...] = jnp.zeros_like(total)

    keys = kv_ref[:, :width]
    values = kv_ref[:, width:]
    allowed = mark_ref[...] == qid_ref[...]
    for head in range(heads):
        scores = jnp.where(allowed, dot(keys, qm[head], NT), -1e30)
        before = top[head : head + 1]
        after = jnp.maximum(before, jnp.max(scores, axis=0, keepdims=True))
        weights = jnp.exp(scores - after)
        fade = jnp.exp(before - after)
        top[head : head + 1] = after
        total[head : head + 1] = total[head : head + 1] * fade + jnp.sum(weights, axis=0, keepdims=True)
        rows = slice(head * HEAD_DIM, (head + 1) * HEAD_DIM)
        part = dot(values, weights.astype(BF16), TN)
        acc[rows] = acc[rows] * fade + part[rows]

    @pl.when(step == pl.num_programs(0) - 1)
    def _():
        scale = 1.0 / total[:heads]
        parts = [
            acc[head * HEAD_DIM : (head + 1) * HEAD_DIM] * scale[head : head + 1] for head in range(heads)
        ]
        out_ref[...] = jnp.concatenate(parts, axis=0).T
        lse_ref[...] = top[...] + jnp.log(jnp.maximum(total[...], 1e-30))


def attention_backward_kernel(
    q_ref, kv_ref, qid_ref, mark_ref, out_ref, lse_ref, do_ref, dq_ref, dkv_ref, qm, dom, acc, delta
):
    step = pl.program_id(0)
    heads = qm.shape[0]
    width = q_ref.shape[1]

    @pl.when(step == 0)
    def _():
        scaled = q_ref[...] * jnp.asarray(0.125, BF16)
        incoming = do_ref[...]
        for head in range(heads):
            qm[head] = head_lanes(scaled, head)
            dom[head] = head_lanes(incoming, head)
        product = incoming.astype(F32) * out_ref[...]
        row = lax.broadcasted_iota(jnp.int32, (8, width), 0)
        lane = lax.broadcasted_iota(jnp.int32, (8, width), 1)
        chooser = jnp.where(lane // HEAD_DIM == row, 1.0, 0.0).astype(F32)
        delta[...] = lax.dot_general(
            chooser, product, NT, preferred_element_type=F32, precision=lax.Precision.HIGHEST
        )
        acc[...] = jnp.zeros_like(acc)

    keys = kv_ref[:, :width]
    values = kv_ref[:, width:]
    allowed = mark_ref[...] == qid_ref[...]
    grad_keys = jnp.zeros(keys.shape, F32)
    grad_values = jnp.zeros(keys.shape, F32)
    for head in range(heads):
        scores = dot(keys, qm[head], NT)
        weights = jnp.where(allowed, jnp.exp(scores - lse_ref[head : head + 1]), 0.0)
        grad_weights = dot(values, dom[head], NT)
        grad_scores = (weights * (grad_weights - delta[head : head + 1])).astype(BF16)
        grad_values += dot(weights.astype(BF16), dom[head])
        grad_keys += dot(grad_scores, qm[head])
        rows = slice(head * HEAD_DIM, (head + 1) * HEAD_DIM)
        acc[rows] += dot(keys, grad_scores, TN)[rows]
    dkv_ref[:, :width] = grad_keys.astype(BF16)
    dkv_ref[:, width:] = grad_values.astype(BF16)

    @pl.when(step == pl.num_programs(0) - 1)
    def _():
        dq_ref[...] = (acc[...] * 0.125).T.astype(BF16)


def key_block(count):
    return 256 if count % 256 == 0 else count


def whole(shape):
    return pl.BlockSpec(shape, lambda step: (0,) * len(shape))


def attention_cost(rows, count, width, products):
    return pl.CostEstimate(
        flops=products * 2 * rows * count * width,
        bytes_accessed=rows * width * 12 + count * width * 8,
        transcendentals=rows * count * (width // HEAD_DIM),
    )


def attention_forward(queries, pairs, query_ids, marks):
    rows, width = queries.shape
    count = pairs.shape[0]
    heads = width // HEAD_DIM
    block = key_block(count)
    return pl.pallas_call(
        attention_forward_kernel,
        grid=(count // block,),
        in_specs=[
            whole((rows, width)),
            pl.BlockSpec((block, 2 * width), lambda step: (step, 0)),
            whole((1, rows)),
            pl.BlockSpec((block, 1), lambda step: (step, 0)),
        ],
        out_specs=[whole((rows, width)), whole((8, rows))],
        out_shape=[
            jax.ShapeDtypeStruct((rows, width), F32),
            jax.ShapeDtypeStruct((8, rows), F32),
        ],
        scratch_shapes=[
            pltpu.VMEM((heads, rows, width), BF16),
            pltpu.VMEM((width, rows), F32),
            pltpu.VMEM((8, rows), F32),
            pltpu.VMEM((8, rows), F32),
        ],
        compiler_params=pltpu.CompilerParams(vmem_limit_bytes=VMEM_LIMIT),
        cost_estimate=attention_cost(rows, count, width, 2),
        name="attention_forward",
    )(queries, pairs, query_ids, marks)


def attention_backward(queries, pairs, query_ids, marks, out, lse, grad_out):
    rows, width = queries.shape
    count = pairs.shape[0]
    heads = width // HEAD_DIM
    block = key_block(count)
    return pl.pallas_call(
        attention_backward_kernel,
        grid=(count // block,),
        in_specs=[
            whole((rows, width)),
            pl.BlockSpec((block, 2 * width), lambda step: (step, 0)),
            whole((1, rows)),
            pl.BlockSpec((block, 1), lambda step: (step, 0)),
            whole((rows, width)),
            whole((8, rows)),
            whole((rows, width)),
        ],
        out_specs=[
            whole((rows, width)),
            pl.BlockSpec((block, 2 * width), lambda step: (step, 0)),
        ],
        out_shape=[
            jax.ShapeDtypeStruct((rows, width), BF16),
            jax.ShapeDtypeStruct((count, 2 * width), BF16),
        ],
        scratch_shapes=[
            pltpu.VMEM((heads, rows, width), BF16),
            pltpu.VMEM((heads, rows, width), BF16),
            pltpu.VMEM((width, rows), F32),
            pltpu.VMEM((8, rows), F32),
        ],
        compiler_params=pltpu.CompilerParams(vmem_limit_bytes=VMEM_LIMIT),
        cost_estimate=attention_cost(rows, count, width, 5),
        name="attention_backward",
    )(queries, pairs, query_ids, marks, out, lse, grad_out)


def norm_forward(value, gain, shift):
    centre = value - jnp.mean(value, axis=-1, keepdims=True)
    inverse = lax.rsqrt(jnp.mean(centre * centre, axis=-1, keepdims=True) + 1e-05)
    unit = centre * inverse
    return unit * gain + shift, unit, inverse


def norm_backward(grad, unit, inverse, gain):
    scaled = grad * gain
    mean_one = jnp.mean(scaled, axis=-1, keepdims=True)
    mean_two = jnp.mean(scaled * unit, axis=-1, keepdims=True)
    return (
        inverse * (scaled - mean_one - unit * mean_two),
        jnp.sum(grad * unit, axis=0),
        jnp.sum(grad, axis=0),
    )


def body(
    tokens,
    cotangent,
    doc_ids,
    pad_mask,
    w_query,
    w_key,
    w_value,
    w_out,
    b_query,
    b_value,
    b_out,
    gain_attn,
    bias_attn,
    w_up,
    b_up,
    w_down,
    b_down,
    gain_ffn,
    bias_ffn,
):
    section = lax.axis_index("section")
    head_count = lax.axis_size("head")
    blk_count = lax.axis_size("blk")
    head_at = lax.axis_index("head")
    blk_at = lax.axis_index("blk")
    batches, rows, width = tokens.shape
    shard = width // (head_count * blk_count)
    hidden_width = w_up.shape[2]
    chunks = hidden_width // width
    half = blk_count // 2
    middles = blk_count // 4
    per_section = batches // 2
    members = 4
    part_width = width // members
    pair_width = 2 * part_width
    first_section = section == 0
    low_half = blk_at < half
    member = (head_at // 2) * 2 + blk_at % 2
    own_batch = section * per_section + blk_at // half
    other_batch = section * per_section + 1 - blk_at // half

    def across_section(value):
        return lax.ppermute(value, "section", [(0, 1), (1, 0)])

    def across_half(value):
        return lax.ppermute(value, "blk", [(at, (at + half) % blk_count) for at in range(blk_count)])

    def across_member(value, step):
        pairs = []
        for head in range(head_count):
            for blk in range(blk_count):
                there = (head ^ (step & 2)) * blk_count + (blk ^ (step & 1))
                pairs.append((head * blk_count + blk, there))
        return lax.ppermute(value, GROUP, pairs)

    def across_core(value):
        return lax.ppermute(value, "head", [(at, at ^ 1) for at in range(head_count)])

    def across_middle(value, step):
        pairs = []
        for at in range(blk_count):
            base, middle, low = at // half, (at % half) // 2, at % 2
            pairs.append((at, base * half + ((middle + step) % middles) * 2 + low))
        return lax.ppermute(value, "blk", pairs)

    def pick(value, at):
        return lax.dynamic_index_in_dim(value, at, 0, keepdims=False)

    def to_heads(groups):
        own = [pick(groups, member ^ step) for step in range(members)]
        return jnp.concatenate(
            [own[0]] + [across_member(own[step], step) for step in range(1, members)], axis=0
        )

    def to_tokens(value):
        parts = value.reshape(members, value.shape[0] // members, value.shape[1])
        back = jnp.stack(
            [parts[0]] + [across_member(parts[step], step) for step in range(1, members)], axis=0
        )
        return [pick(back, member ^ at) for at in range(members)]

    def all_keys(value):
        value = jnp.concatenate([value, across_core(value)], axis=0)
        return jnp.concatenate(
            [value] + [across_middle(value, step) for step in range(1, middles)], axis=0
        )

    def own_keys_sum(value):
        count = value.shape[0] // middles
        total = value[:count].astype(F32)
        for step in range(1, middles):
            back = across_middle(value[step * count : (step + 1) * count], middles - step)
            total = total + back.astype(F32)
        partner = across_core(total[count // 2 :].astype(BF16))
        return (total[: count // 2] + partner.astype(F32)).astype(BF16)

    def columns(value, size):
        return value.reshape(value.shape[0], members, size).transpose(1, 0, 2)

    def split_parts(value):
        return value[0].reshape(shard, members, part_width)

    pairs_local = jnp.concatenate([split_parts(w_key), split_parts(w_value)], axis=2)
    small_local = jnp.stack(
        [
            part.reshape(shard)
            for part in (b_query, b_value, b_out, gain_attn, bias_attn, b_down, gain_ffn, bias_ffn)
        ]
        + [b_up[0].reshape(chunks, shard)[at] for at in range(chunks)],
        axis=1,
    )
    small_count = small_local.shape[1]
    joint_width = 3 * width
    first_local = jnp.concatenate(
        [
            pairs_local.reshape(shard, 2 * width),
            w_query[0],
            jnp.pad(small_local, ((0, 0), (0, 128 - small_count))),
        ],
        axis=1,
    )
    up_local = (
        w_up[0]
        .reshape(shard, head_count * blk_count, chunks, shard)
        .transpose(0, 2, 1, 3)
        .reshape(shard, hidden_width)
    )
    down_local = jnp.concatenate(
        [w_down[0, at * shard : (at + 1) * shard] for at in range(chunks)], axis=1
    )
    rest_local = jnp.concatenate([w_out[0], up_local, down_local], axis=1)
    rest_other = across_section(rest_local)
    first_all = lax.all_gather(first_local, ("section",) + GROUP, axis=0, tiled=True)
    rest_all = [
        lax.all_gather(
            jnp.where(first_section, rest_local, rest_other), GROUP, axis=0, tiled=True
        ),
        lax.all_gather(
            jnp.where(first_section, rest_other, rest_local), GROUP, axis=0, tiled=True
        ),
    ]

    def both_blocks(value):
        return jnp.concatenate(
            [pick(value, own_batch), across_half(pick(value, other_batch))], axis=0
        )

    layer_in = both_blocks(tokens)
    grad_top = both_blocks(cotangent)
    marks_local = jnp.where(pad_mask == 1, doc_ids, -1)
    labels = both_blocks(jnp.stack([doc_ids, marks_local], axis=-1))
    labels = jnp.concatenate(
        [labels] + [across_member(labels, step) for step in range(1, members)], axis=0
    )
    query_ids = labels[:, 0].reshape(1, -1)
    key_marks = all_keys(labels)[:, 1].reshape(-1, 1)

    layers = []
    outputs = []
    for layer in range(2):
        joint = first_all[layer * width : (layer + 1) * width, :joint_width]
        small = first_all[layer * width : (layer + 1) * width, joint_width:].T.astype(F32)
        rest = rest_all[layer]
        out_weight = rest[:, :width]
        up_weight = rest[:, width : width + hidden_width]
        down_weight = [
            rest[:, width + hidden_width + at * width : width + hidden_width + (at + 1) * width]
            for at in range(chunks)
        ]
        q_shift, v_shift, out_shift, gain_one, shift_one, down_shift, gain_two, shift_two = [
            small[at] for at in range(8)
        ]
        up_shift = small[8 : 8 + chunks].reshape(hidden_width)
        pair_shift = jnp.concatenate(
            [jnp.zeros((members, part_width), F32), v_shift.reshape(members, part_width)], axis=1
        )
        joint_shift = jnp.concatenate([pair_shift.reshape(2 * width), q_shift])
        joint_rows = (dot(layer_in, joint) + joint_shift).astype(BF16)
        pairs = all_keys(to_heads(columns(joint_rows[:, : 2 * width], pair_width)))
        queries = to_heads(columns(joint_rows[:, 2 * width :], part_width))
        mixed, lse = attention_forward(queries, pairs, query_ids, key_marks)
        attended = jnp.concatenate(to_tokens(mixed.astype(BF16)), axis=1)
        first_sum = layer_in.astype(F32) + dot(attended, out_weight) + out_shift
        middle, unit_one, inverse_one = norm_forward(first_sum, gain_one, shift_one)
        middle_low = middle.astype(BF16)
        hidden = dot(middle_low, up_weight) + up_shift
        share = 0.5 * lax.erfc(hidden * (-(0.5**0.5)))
        slope = share + hidden * jnp.exp(hidden * hidden * -0.5) * 0.3989422804014327
        active = (hidden * share).astype(BF16)
        second = middle + down_shift
        for at in range(chunks):
            second = second + dot(active[:, at * width : (at + 1) * width], down_weight[at])
        result, unit_two, inverse_two = norm_forward(second, gain_two, shift_two)
        layers.append(
            (
                layer_in,
                joint,
                out_weight,
                up_weight,
                down_weight,
                gain_one,
                gain_two,
                pairs,
                queries,
                mixed,
                lse,
                attended,
                unit_one,
                inverse_one,
                middle_low,
                slope,
                active,
                unit_two,
                inverse_two,
            )
        )
        layer_in = result.astype(BF16)
        outputs.append(layer_in)

    def reduced(value):
        return lax.psum_scatter(value, GROUP, scatter_dimension=0, tiled=True)

    wide_sums = [None, None]
    last_sums = [None, None]
    grads = [None, None]
    for layer in (1, 0):
        (
            layer_in,
            joint,
            out_weight,
            up_weight,
            down_weight,
            gain_one,
            gain_two,
            pairs,
            queries,
            mixed,
            lse,
            attended,
            unit_one,
            inverse_one,
            middle_low,
            slope,
            active,
            unit_two,
            inverse_two,
        ) = layers[layer]
        grad_second, grad_gain_two, grad_shift_two = norm_backward(
            grad_top, unit_two, inverse_two, gain_two
        )
        grad_down_low = grad_second.astype(BF16)
        grad_active = jnp.concatenate(
            [dot(grad_down_low, down_weight[at], NT) for at in range(chunks)], axis=1
        )
        grad_hidden = (grad_active * slope).astype(BF16)
        grad_down = [
            dot(active[:, at * width : (at + 1) * width], grad_down_low, TN).astype(BF16)
            for at in range(chunks)
        ]
        grad_up = dot(middle_low, grad_hidden, TN).astype(BF16)
        wide_sums[layer] = reduced(jnp.concatenate([grad_up] + grad_down, axis=1))
        grad_middle = grad_second + dot(grad_hidden, up_weight, NT)
        grad_first, grad_gain_one, grad_shift_one = norm_backward(
            grad_middle, unit_one, inverse_one, gain_one
        )
        grad_branch = grad_first.astype(BF16)
        grad_out = dot(attended, grad_branch, TN).astype(BF16)
        grad_returned = dot(grad_branch, out_weight, NT).astype(BF16)
        grad_mixed = to_heads(columns(grad_returned, part_width))
        grad_queries, grad_pairs = attention_backward(
            queries, pairs, query_ids, key_marks, mixed, lse, grad_mixed
        )
        pair_parts = to_tokens(own_keys_sum(grad_pairs))
        query_parts = to_tokens(grad_queries)
        grad_joint = jnp.concatenate(pair_parts + query_parts, axis=1)
        grad_joint_weight = dot(layer_in, grad_joint, TN).astype(BF16)
        grad_input = grad_first + dot(grad_joint, joint, NT)
        joint_sum = jnp.sum(grad_joint.astype(F32), axis=0)
        small = jnp.stack(
            [
                joint_sum[2 * width :],
                joint_sum[: 2 * width].reshape(members, 2, part_width)[:, 1].reshape(width),
                jnp.sum(grad_branch.astype(F32), axis=0),
                grad_gain_one,
                grad_shift_one,
                jnp.sum(grad_down_low.astype(F32), axis=0),
                grad_gain_two,
                grad_shift_two,
            ],
            axis=0,
        )
        hidden_sum = jnp.sum(grad_hidden.astype(F32), axis=0).reshape(chunks, width)
        small = jnp.concatenate([small, hidden_sum], axis=0).astype(BF16)
        small = jnp.pad(small.T, ((0, 0), (0, 128 - small_count)))
        last_sums[layer] = reduced(
            jnp.concatenate([grad_joint_weight, grad_out, small], axis=1)
        )
        grads[layer] = grad_input
        grad_top = grad_input.astype(BF16).astype(F32)

    def settle(first, second):
        sent = jnp.where(first_section, second, first)
        kept = jnp.where(first_section, first, second)
        return kept.astype(F32) + across_section(sent).astype(F32)

    wide = settle(wide_sums[0], wide_sums[1])
    last = settle(last_sums[0], last_sums[1])
    grad_up = (
        wide[:, :hidden_width]
        .reshape(shard, chunks, head_count * blk_count, shard)
        .transpose(0, 2, 1, 3)
        .reshape(shard, hidden_width)
    )
    grad_down = jnp.concatenate(
        [
            wide[:, hidden_width + at * width : hidden_width + (at + 1) * width]
            for at in range(chunks)
        ],
        axis=0,
    )
    grad_pairs = last[:, : 2 * width].reshape(shard, members, 2, part_width)
    grad_key = grad_pairs[:, :, 0].reshape(shard, width)
    grad_value = grad_pairs[:, :, 1].reshape(shard, width)
    grad_query = last[:, 2 * width : 3 * width]
    grad_out = last[:, 3 * width : 4 * width]
    small = last[:, 4 * width :].T

    def placed_rows(first, second):
        def halves(value):
            got = across_half(value[rows:])
            own = value[:rows]
            return jnp.stack([jnp.where(low_half, own, got), jnp.where(low_half, got, own)], axis=0)

        first, second = halves(first), halves(second)
        got = across_section(jnp.where(first_section, second, first))
        kept = jnp.where(first_section, first, second)
        return jnp.where(
            first_section,
            jnp.concatenate([kept, got], axis=0),
            jnp.concatenate([got, kept], axis=0),
        )

    outputs_all = placed_rows(outputs[0], outputs[1])
    grad_inputs = placed_rows(grads[0], grads[1])
    return (
        outputs_all[None],
        grad_inputs[None],
        grad_query[None],
        grad_key[None],
        grad_value[None],
        grad_out[None],
        small[0][None],
        small[1][None],
        small[2][None],
        small[3][None],
        small[4][None],
        grad_up[None],
        small[8 : 8 + chunks].reshape(1, chunks * shard),
        grad_down[None],
        small[5][None],
        small[6][None],
        small[7][None],
    )


def solution(mesh):
    rows = P(None, GROUP, None)
    marks = P(None, GROUP)
    matrix = P("section", GROUP, None)
    vector = P("section", GROUP)
    result = P("section", None, GROUP, None)
    return jax.shard_map(
        body,
        mesh=mesh,
        in_specs=(rows, rows, marks, marks)
        + (matrix,) * 4
        + (vector,) * 5
        + (matrix, vector, matrix, vector, vector, vector),
        out_specs=(result, result)
        + (matrix,) * 4
        + (vector,) * 5
        + (matrix, vector, matrix, vector, vector, vector),
        check_vma=False,
    )
```

```python
import functools

import jax
import jax.numpy as jnp
from jax import lax
from jax.experimental import pallas as pl
from jax.experimental.pallas import tpu as pltpu
from jax.sharding import PartitionSpec as P

HEAD_DIM = 64
GROUP = ("head", "blk")
F32 = jnp.float32
BF16 = jnp.bfloat16
NT = (((1,), (1,)), ((), ()))
NN = (((1,), (0,)), ((), ()))
TN = (((0,), (0,)), ((), ()))
VMEM_LIMIT = 48 * 1024 * 1024


def dot(left, right, dims=NN):
    return lax.dot_general(left, right, dims, preferred_element_type=F32)


def head_lanes(value, head):
    lane = lax.broadcasted_iota(jnp.int32, value.shape, 1)
    return jnp.where(lane // HEAD_DIM == head, value, jnp.zeros_like(value))


def attention_forward_kernel(q_ref, kv_ref, qid_ref, mark_ref, out_ref, lse_ref, qm, acc, top, total):
    step = pl.program_id(0)
    heads = qm.shape[0]
    width = q_ref.shape[1]

    @pl.when(step == 0)
    def _():
        scaled = q_ref[...] * jnp.asarray(0.125, BF16)
        for head in range(heads):
            qm[head] = head_lanes(scaled, head)
        acc[...] = jnp.zeros_like(acc)
        top[...] = jnp.full_like(top, -1e30)
        total[...] = jnp.zeros_like(total)

    keys = kv_ref[:, :width]
    values = kv_ref[:, width:]
    allowed = mark_ref[...] == qid_ref[...]
    for head in range(heads):
        scores = jnp.where(allowed, dot(keys, qm[head], NT), -1e30)
        before = top[head : head + 1]
        after = jnp.maximum(before, jnp.max(scores, axis=0, keepdims=True))
        weights = jnp.exp(scores - after)
        fade = jnp.exp(before - after)
        top[head : head + 1] = after
        total[head : head + 1] = total[head : head + 1] * fade + jnp.sum(weights, axis=0, keepdims=True)
        rows = slice(head * HEAD_DIM, (head + 1) * HEAD_DIM)
        part = dot(values, weights.astype(BF16), TN)
        acc[rows] = acc[rows] * fade + part[rows]

    @pl.when(step == pl.num_programs(0) - 1)
    def _():
        scale = 1.0 / total[:heads]
        parts = [
            acc[head * HEAD_DIM : (head + 1) * HEAD_DIM] * scale[head : head + 1] for head in range(heads)
        ]
        out_ref[...] = jnp.concatenate(parts, axis=0).T
        lse_ref[...] = top[...] + jnp.log(jnp.maximum(total[...], 1e-30))


def attention_backward_kernel(
    q_ref, kv_ref, qid_ref, mark_ref, out_ref, lse_ref, do_ref, dq_ref, dkv_ref, qm, dom, acc, delta
):
    step = pl.program_id(0)
    heads = qm.shape[0]
    width = q_ref.shape[1]

    @pl.when(step == 0)
    def _():
        scaled = q_ref[...] * jnp.asarray(0.125, BF16)
        incoming = do_ref[...]
        for head in range(heads):
            qm[head] = head_lanes(scaled, head)
            dom[head] = head_lanes(incoming, head)
        product = incoming.astype(F32) * out_ref[...]
        row = lax.broadcasted_iota(jnp.int32, (8, width), 0)
        lane = lax.broadcasted_iota(jnp.int32, (8, width), 1)
        chooser = jnp.where(lane // HEAD_DIM == row, 1.0, 0.0).astype(F32)
        delta[...] = lax.dot_general(
            chooser, product, NT, preferred_element_type=F32, precision=lax.Precision.HIGHEST
        )
        acc[...] = jnp.zeros_like(acc)

    keys = kv_ref[:, :width]
    values = kv_ref[:, width:]
    allowed = mark_ref[...] == qid_ref[...]
    grad_keys = jnp.zeros(keys.shape, F32)
    grad_values = jnp.zeros(keys.shape, F32)
    for head in range(heads):
        scores = dot(keys, qm[head], NT)
        weights = jnp.where(allowed, jnp.exp(scores - lse_ref[head : head + 1]), 0.0)
        grad_weights = dot(values, dom[head], NT)
        grad_scores = (weights * (grad_weights - delta[head : head + 1])).astype(BF16)
        grad_values += dot(weights.astype(BF16), dom[head])
        grad_keys += dot(grad_scores, qm[head])
        rows = slice(head * HEAD_DIM, (head + 1) * HEAD_DIM)
        acc[rows] += dot(keys, grad_scores, TN)[rows]
    dkv_ref[:, :width] = grad_keys.astype(BF16)
    dkv_ref[:, width:] = grad_values.astype(BF16)

    @pl.when(step == pl.num_programs(0) - 1)
    def _():
        dq_ref[...] = (acc[...] * 0.125).T.astype(BF16)


def key_block(count):
    return 256 if count % 256 == 0 else count


def whole(shape):
    return pl.BlockSpec(shape, lambda step: (0,) * len(shape))


def attention_cost(rows, count, width, products):
    return pl.CostEstimate(
        flops=products * 2 * rows * count * width,
        bytes_accessed=rows * width * 12 + count * width * 8,
        transcendentals=rows * count * (width // HEAD_DIM),
    )


def attention_forward(queries, pairs, query_ids, marks):
    rows, width = queries.shape
    count = pairs.shape[0]
    heads = width // HEAD_DIM
    block = key_block(count)
    return pl.pallas_call(
        attention_forward_kernel,
        grid=(count // block,),
        in_specs=[
            whole((rows, width)),
            pl.BlockSpec((block, 2 * width), lambda step: (step, 0)),
            whole((1, rows)),
            pl.BlockSpec((block, 1), lambda step: (step, 0)),
        ],
        out_specs=[whole((rows, width)), whole((8, rows))],
        out_shape=[
            jax.ShapeDtypeStruct((rows, width), F32),
            jax.ShapeDtypeStruct((8, rows), F32),
        ],
        scratch_shapes=[
            pltpu.VMEM((heads, rows, width), BF16),
            pltpu.VMEM((width, rows), F32),
            pltpu.VMEM((8, rows), F32),
            pltpu.VMEM((8, rows), F32),
        ],
        compiler_params=pltpu.CompilerParams(vmem_limit_bytes=VMEM_LIMIT),
        cost_estimate=attention_cost(rows, count, width, 2),
        name="attention_forward",
    )(queries, pairs, query_ids, marks)


def attention_backward(queries, pairs, query_ids, marks, out, lse, grad_out):
    rows, width = queries.shape
    count = pairs.shape[0]
    heads = width // HEAD_DIM
    block = key_block(count)
    return pl.pallas_call(
        attention_backward_kernel,
        grid=(count // block,),
        in_specs=[
            whole((rows, width)),
            pl.BlockSpec((block, 2 * width), lambda step: (step, 0)),
            whole((1, rows)),
            pl.BlockSpec((block, 1), lambda step: (step, 0)),
            whole((rows, width)),
            whole((8, rows)),
            whole((rows, width)),
        ],
        out_specs=[
            whole((rows, width)),
            pl.BlockSpec((block, 2 * width), lambda step: (step, 0)),
        ],
        out_shape=[
            jax.ShapeDtypeStruct((rows, width), BF16),
            jax.ShapeDtypeStruct((count, 2 * width), BF16),
        ],
        scratch_shapes=[
            pltpu.VMEM((heads, rows, width), BF16),
            pltpu.VMEM((heads, rows, width), BF16),
            pltpu.VMEM((width, rows), F32),
            pltpu.VMEM((8, rows), F32),
        ],
        compiler_params=pltpu.CompilerParams(vmem_limit_bytes=VMEM_LIMIT),
        cost_estimate=attention_cost(rows, count, width, 5),
        name="attention_backward",
    )(queries, pairs, query_ids, marks, out, lse, grad_out)


def norm_forward(value, gain, shift):
    centre = value - jnp.mean(value, axis=-1, keepdims=True)
    inverse = lax.rsqrt(jnp.mean(centre * centre, axis=-1, keepdims=True) + 1e-05)
    unit = centre * inverse
    return unit * gain + shift, unit, inverse


def norm_backward(grad, unit, inverse, gain):
    scaled = grad * gain
    mean_one = jnp.mean(scaled, axis=-1, keepdims=True)
    mean_two = jnp.mean(scaled * unit, axis=-1, keepdims=True)
    return (
        inverse * (scaled - mean_one - unit * mean_two),
        jnp.sum(grad * unit, axis=0),
        jnp.sum(grad, axis=0),
    )


def body(
    tokens,
    cotangent,
    doc_ids,
    pad_mask,
    w_query,
    w_key,
    w_value,
    w_out,
    b_query,
    b_value,
    b_out,
    gain_attn,
    bias_attn,
    w_up,
    b_up,
    w_down,
    b_down,
    gain_ffn,
    bias_ffn,
):
    section = lax.axis_index("section")
    head_count = lax.axis_size("head")
    blk_count = lax.axis_size("blk")
    head_at = lax.axis_index("head")
    blk_at = lax.axis_index("blk")
    batches, rows, width = tokens.shape
    shard = width // (head_count * blk_count)
    hidden_width = w_up.shape[2]
    chunks = hidden_width // width
    half = blk_count // 2
    middles = blk_count // 4
    per_section = batches // 2
    members = 4
    part_width = width // members
    pair_width = 2 * part_width
    first_section = section == 0
    low_half = blk_at < half
    member = (head_at // 2) * 2 + blk_at % 2
    own_batch = section * per_section + blk_at // half
    other_batch = section * per_section + 1 - blk_at // half

    def across_section(value):
        return lax.ppermute(value, "section", [(0, 1), (1, 0)])

    def across_half(value):
        return lax.ppermute(value, "blk", [(at, (at + half) % blk_count) for at in range(blk_count)])

    def across_member(value, step):
        pairs = []
        for head in range(head_count):
            for blk in range(blk_count):
                there = (head ^ (step & 2)) * blk_count + (blk ^ (step & 1))
                pairs.append((head * blk_count + blk, there))
        return lax.ppermute(value, GROUP, pairs)

    def across_core(value):
        return lax.ppermute(value, "head", [(at, at ^ 1) for at in range(head_count)])

    def across_middle(value, step):
        pairs = []
        for at in range(blk_count):
            base, middle, low = at // half, (at % half) // 2, at % 2
            pairs.append((at, base * half + ((middle + step) % middles) * 2 + low))
        return lax.ppermute(value, "blk", pairs)

    direct = head_count == 4 and blk_count == 4
    core_at = head_at % 2
    side_at = head_at // 2

    def across_side(value):
        return lax.ppermute(value, "head", [(at, at ^ 2) for at in range(head_count)])

    def add(left, right):
        return (left.astype(F32) + right.astype(F32)).astype(BF16)

    def side_sum(value):
        kept = lax.dynamic_index_in_dim(value, side_at, 1, keepdims=False)
        sent = lax.dynamic_index_in_dim(value, 1 - side_at, 1, keepdims=False)
        return add(kept, across_side(sent))

    def line_sum(value, axis):
        def entry(at):
            return lax.dynamic_index_in_dim(value, jnp.clip(at, 0, blk_count - 1), axis, keepdims=False)

        right = [(at, at + 1) for at in range(blk_count - 1)]
        left = [(at + 1, at) for at in range(blk_count - 1)]
        from_left = from_right = None
        for step in range(1, blk_count):
            to_right = entry(blk_at + blk_count - step)
            to_left = entry(blk_at - blk_count + step)
            if step > 1:
                to_right = add(to_right, from_left)
                to_left = add(to_left, from_right)
            from_left = lax.ppermute(to_right, "blk", right)
            from_right = lax.ppermute(to_left, "blk", left)
        return entry(blk_at).astype(F32) + from_left.astype(F32) + from_right.astype(F32)

    def chip_sum(kept, sent, side_first):
        value = add(kept, across_core(sent))
        if side_first:
            return line_sum(side_sum(value), 1)
        return side_sum(line_sum(value, 2).astype(BF16))

    def halves(value, axis):
        shape = value.shape
        lead = shape[axis] // width
        split = value.reshape(shape[:axis] + (lead, 2, 2, width // 4) + shape[axis + 1 :])
        first = lax.index_in_dim(split, 0, axis + 2, keepdims=False)
        second = lax.index_in_dim(split, 1, axis + 2, keepdims=False)
        flat = shape[:axis] + (shape[axis] // 2,) + shape[axis + 1 :]
        return (
            jnp.where(core_at == 0, first, second).reshape(flat),
            jnp.where(core_at == 0, second, first).reshape(flat),
        )

    def scattered(kept, sent, side_first):
        shape = (-1, 2, blk_count, shard, kept.shape[-1])
        return chip_sum(kept.reshape(shape), sent.reshape(shape), side_first)

    def weight_grad(left, right):
        if not direct:
            return (dot(left, right, TN).astype(BF16),)
        kept, sent = halves(left, 1)
        return (dot(kept, right, TN).astype(BF16), dot(sent, right, TN).astype(BF16))

    def reduced(parts, side_first):
        if not direct:
            value = parts[0].reshape(-1, width, parts[0].shape[-1])
            return lax.psum_scatter(value, GROUP, scatter_dimension=1, tiled=True)
        return scattered(parts[0], parts[1], side_first)

    def pick(value, at):
        return lax.dynamic_index_in_dim(value, at, 0, keepdims=False)

    def to_heads(groups):
        own = [pick(groups, member ^ step) for step in range(members)]
        return jnp.concatenate(
            [own[0]] + [across_member(own[step], step) for step in range(1, members)], axis=0
        )

    def to_tokens(value):
        parts = value.reshape(members, value.shape[0] // members, value.shape[1])
        back = jnp.stack(
            [parts[0]] + [across_member(parts[step], step) for step in range(1, members)], axis=0
        )
        return [pick(back, member ^ at) for at in range(members)]

    def all_keys(value):
        value = jnp.concatenate([value, across_core(value)], axis=0)
        return jnp.concatenate(
            [value] + [across_middle(value, step) for step in range(1, middles)], axis=0
        )

    def own_keys_sum(value):
        count = value.shape[0] // middles
        total = value[:count].astype(F32)
        for step in range(1, middles):
            back = across_middle(value[step * count : (step + 1) * count], middles - step)
            total = total + back.astype(F32)
        partner = across_core(total[count // 2 :].astype(BF16))
        return (total[: count // 2] + partner.astype(F32)).astype(BF16)

    def columns(value, size):
        return value.reshape(value.shape[0], members, size).transpose(1, 0, 2)

    def split_parts(value):
        return value[0].reshape(shard, members, part_width)

    pairs_local = jnp.concatenate([split_parts(w_key), split_parts(w_value)], axis=2)
    small_local = jnp.stack(
        [
            part.reshape(shard)
            for part in (b_query, b_value, b_out, gain_attn, bias_attn, b_down, gain_ffn, bias_ffn)
        ]
        + [b_up[0].reshape(chunks, shard)[at] for at in range(chunks)],
        axis=1,
    )
    small_count = small_local.shape[1]
    joint_width = 3 * width
    first_local = jnp.concatenate(
        [
            pairs_local.reshape(shard, 2 * width),
            w_query[0],
            jnp.pad(small_local, ((0, 0), (0, 128 - small_count))),
        ],
        axis=1,
    )
    up_local = (
        w_up[0]
        .reshape(shard, head_count * blk_count, chunks, shard)
        .transpose(0, 2, 1, 3)
        .reshape(shard, hidden_width)
    )
    down_local = jnp.concatenate(
        [w_down[0, at * shard : (at + 1) * shard] for at in range(chunks)], axis=1
    )
    rest_local = jnp.concatenate([w_out[0], up_local, down_local], axis=1)
    rest_other = across_section(rest_local)
    first_all = lax.all_gather(first_local, ("section",) + GROUP, axis=0, tiled=True)
    rest_all = [
        lax.all_gather(
            jnp.where(first_section, rest_local, rest_other), GROUP, axis=0, tiled=True
        ),
        lax.all_gather(
            jnp.where(first_section, rest_other, rest_local), GROUP, axis=0, tiled=True
        ),
    ]

    def both_blocks(value):
        return jnp.concatenate(
            [pick(value, own_batch), across_half(pick(value, other_batch))], axis=0
        )

    layer_in = both_blocks(tokens)
    grad_top = both_blocks(cotangent)
    marks_local = jnp.where(pad_mask == 1, doc_ids, -1)
    labels = both_blocks(jnp.stack([doc_ids, marks_local], axis=-1))
    labels = jnp.concatenate(
        [labels] + [across_member(labels, step) for step in range(1, members)], axis=0
    )
    query_ids = labels[:, 0].reshape(1, -1)
    key_marks = all_keys(labels)[:, 1].reshape(-1, 1)

    layers = []
    outputs = []
    for layer in range(2):
        joint = first_all[layer * width : (layer + 1) * width, :joint_width]
        small = first_all[layer * width : (layer + 1) * width, joint_width:].T.astype(F32)
        rest = rest_all[layer]
        out_weight = rest[:, :width]
        up_weight = rest[:, width : width + hidden_width]
        down_weight = [
            rest[:, width + hidden_width + at * width : width + hidden_width + (at + 1) * width]
            for at in range(chunks)
        ]
        q_shift, v_shift, out_shift, gain_one, shift_one, down_shift, gain_two, shift_two = [
            small[at] for at in range(8)
        ]
        up_shift = small[8 : 8 + chunks].reshape(hidden_width)
        pair_shift = jnp.concatenate(
            [jnp.zeros((members, part_width), F32), v_shift.reshape(members, part_width)], axis=1
        )
        joint_shift = jnp.concatenate([pair_shift.reshape(2 * width), q_shift])
        joint_rows = (dot(layer_in, joint) + joint_shift).astype(BF16)
        pairs = all_keys(to_heads(columns(joint_rows[:, : 2 * width], pair_width)))
        queries = to_heads(columns(joint_rows[:, 2 * width :], part_width))
        mixed, lse = attention_forward(queries, pairs, query_ids, key_marks)
        attended = jnp.concatenate(to_tokens(mixed.astype(BF16)), axis=1)
        first_sum = layer_in.astype(F32) + dot(attended, out_weight) + out_shift
        middle, unit_one, inverse_one = norm_forward(first_sum, gain_one, shift_one)
        middle_low = middle.astype(BF16)
        hidden = dot(middle_low, up_weight) + up_shift
        share = 0.5 * lax.erfc(hidden * (-(0.5**0.5)))
        slope = share + hidden * jnp.exp(hidden * hidden * -0.5) * 0.3989422804014327
        active = (hidden * share).astype(BF16)
        second = middle + down_shift
        for at in range(chunks):
            second = second + dot(active[:, at * width : (at + 1) * width], down_weight[at])
        result, unit_two, inverse_two = norm_forward(second, gain_two, shift_two)
        layers.append(
            (
                layer_in,
                joint,
                out_weight,
                up_weight,
                down_weight,
                gain_one,
                gain_two,
                pairs,
                queries,
                mixed,
                lse,
                attended,
                unit_one,
                inverse_one,
                middle_low,
                slope,
                active,
                unit_two,
                inverse_two,
            )
        )
        layer_in = result.astype(BF16)
        outputs.append(layer_in)

    sums = [None, None]
    grads = [None, None]
    for layer in (1, 0):
        (
            layer_in,
            joint,
            out_weight,
            up_weight,
            down_weight,
            gain_one,
            gain_two,
            pairs,
            queries,
            mixed,
            lse,
            attended,
            unit_one,
            inverse_one,
            middle_low,
            slope,
            active,
            unit_two,
            inverse_two,
        ) = layers[layer]
        grad_second, grad_gain_two, grad_shift_two = norm_backward(
            grad_top, unit_two, inverse_two, gain_two
        )
        grad_down_low = grad_second.astype(BF16)
        grad_active = jnp.concatenate(
            [dot(grad_down_low, down_weight[at], NT) for at in range(chunks)], axis=1
        )
        grad_hidden = (grad_active * slope).astype(BF16)
        up_parts = weight_grad(middle_low, grad_hidden)
        down_parts = weight_grad(active, grad_down_low)
        grad_hidden, up_parts, down_parts = lax.optimization_barrier(
            (grad_hidden, up_parts, down_parts)
        )
        up_sum = reduced(up_parts, True)
        down_sum = reduced(down_parts, False)
        grad_middle = grad_second + dot(grad_hidden, up_weight, NT)
        grad_first, grad_gain_one, grad_shift_one = norm_backward(
            grad_middle, unit_one, inverse_one, gain_one
        )
        grad_branch = grad_first.astype(BF16)
        out_parts = weight_grad(attended, grad_branch)
        out_sum = reduced(out_parts, False)
        grad_returned = dot(grad_branch, out_weight, NT).astype(BF16)
        grad_mixed = to_heads(columns(grad_returned, part_width))
        grad_queries, grad_pairs = attention_backward(
            queries, pairs, query_ids, key_marks, mixed, lse, grad_mixed
        )
        pair_parts = to_tokens(own_keys_sum(grad_pairs))
        query_parts = to_tokens(grad_queries)
        grad_joint = jnp.concatenate(pair_parts + query_parts, axis=1)
        joint_parts = weight_grad(layer_in, grad_joint)
        grad_input = grad_first + dot(grad_joint, joint, NT)
        joint_sum = jnp.sum(grad_joint.astype(F32), axis=0)
        small = jnp.stack(
            [
                joint_sum[2 * width :],
                joint_sum[: 2 * width].reshape(members, 2, part_width)[:, 1].reshape(width),
                jnp.sum(grad_branch.astype(F32), axis=0),
                grad_gain_one,
                grad_shift_one,
                jnp.sum(grad_down_low.astype(F32), axis=0),
                grad_gain_two,
                grad_shift_two,
            ],
            axis=0,
        )
        hidden_sum = jnp.sum(grad_hidden.astype(F32), axis=0).reshape(chunks, width)
        small = jnp.concatenate([small, hidden_sum], axis=0).astype(BF16)
        small = jnp.pad(small.T, ((0, 0), (0, 128 - small_count)))
        joint_sum = reduced(joint_parts, True)
        small_sum = reduced(halves(small, 0) if direct else (small,), False)
        sums[layer] = [up_sum, down_sum, out_sum, joint_sum, small_sum]
        grads[layer] = grad_input
        grad_top = grad_input.astype(BF16).astype(F32)

    def settle(first, second):
        to_first = lax.ppermute(first.astype(BF16), "section", [(1, 0)])
        to_second = lax.ppermute(second.astype(BF16), "section", [(0, 1)])
        return jnp.where(
            first_section,
            first.astype(F32) + to_first.astype(F32),
            second.astype(F32) + to_second.astype(F32),
        )

    wide, down, out, last, small = [settle(first, second) for first, second in zip(*sums)]
    grad_up = (
        wide.reshape(shard, chunks, head_count * blk_count, shard)
        .transpose(0, 2, 1, 3)
        .reshape(shard, hidden_width)
    )
    grad_down = down.reshape(chunks * shard, width)
    grad_pairs = last[0, :, : 2 * width].reshape(shard, members, 2, part_width)
    grad_key = grad_pairs[:, :, 0].reshape(shard, width)
    grad_value = grad_pairs[:, :, 1].reshape(shard, width)
    grad_query = last[0, :, 2 * width :]
    grad_out = out[0]
    small = small[0].T

    def placed_rows(first, second):
        def halves(value):
            got = across_half(value[rows:])
            own = value[:rows]
            return jnp.stack([jnp.where(low_half, own, got), jnp.where(low_half, got, own)], axis=0)

        first, second = halves(first), halves(second)
        got = across_section(jnp.where(first_section, second, first))
        kept = jnp.where(first_section, first, second)
        return jnp.where(
            first_section,
            jnp.concatenate([kept, got], axis=0),
            jnp.concatenate([got, kept], axis=0),
        )

    outputs_all = placed_rows(outputs[0], outputs[1])
    grad_inputs = placed_rows(grads[0], grads[1])
    return (
        outputs_all[None],
        grad_inputs[None],
        grad_query[None],
        grad_key[None],
        grad_value[None],
        grad_out[None],
        small[0][None],
        small[1][None],
        small[2][None],
        small[3][None],
        small[4][None],
        grad_up[None],
        small[8 : 8 + chunks].reshape(1, chunks * shard),
        grad_down[None],
        small[5][None],
        small[6][None],
        small[7][None],
    )


def solution(mesh):
    rows = P(None, GROUP, None)
    marks = P(None, GROUP)
    matrix = P("section", GROUP, None)
    vector = P("section", GROUP)
    result = P("section", None, GROUP, None)
    return jax.shard_map(
        body,
        mesh=mesh,
        in_specs=(rows, rows, marks, marks)
        + (matrix,) * 4
        + (vector,) * 5
        + (matrix, vector, matrix, vector, vector, vector),
        out_specs=(result, result)
        + (matrix,) * 4
        + (vector,) * 5
        + (matrix, vector, matrix, vector, vector, vector),
        check_vma=False,
    )
```

```python
import functools

import jax
import jax.numpy as jnp
from jax import lax
from jax.experimental import pallas as pl
from jax.experimental.pallas import tpu as pltpu
from jax.sharding import PartitionSpec as P

HEAD_DIM = 64
GROUP = ("head", "blk")
F32 = jnp.float32
BF16 = jnp.bfloat16
NT = (((1,), (1,)), ((), ()))
NN = (((1,), (0,)), ((), ()))
TN = (((0,), (0,)), ((), ()))
VMEM_LIMIT = 48 * 1024 * 1024


def dot(left, right, dims=NN):
    return lax.dot_general(left, right, dims, preferred_element_type=F32)


def head_lanes(value, head):
    lane = lax.broadcasted_iota(jnp.int32, value.shape, 1)
    return jnp.where(lane // HEAD_DIM == head, value, jnp.zeros_like(value))


def attention_forward_kernel(q_ref, kv_ref, qid_ref, mark_ref, out_ref, lse_ref, qm, acc, top, total):
    step = pl.program_id(0)
    heads = qm.shape[0]
    width = q_ref.shape[1]

    @pl.when(step == 0)
    def _():
        scaled = q_ref[...] * jnp.asarray(0.125, BF16)
        for head in range(heads):
            qm[head] = head_lanes(scaled, head)
        acc[...] = jnp.zeros_like(acc)
        top[...] = jnp.full_like(top, -1e30)
        total[...] = jnp.zeros_like(total)

    keys = kv_ref[:, :width]
    values = kv_ref[:, width:]
    allowed = mark_ref[...] == qid_ref[...]
    for head in range(heads):
        scores = jnp.where(allowed, dot(keys, qm[head], NT), -1e30)
        before = top[head : head + 1]
        after = jnp.maximum(before, jnp.max(scores, axis=0, keepdims=True))
        weights = jnp.exp(scores - after)
        fade = jnp.exp(before - after)
        top[head : head + 1] = after
        total[head : head + 1] = total[head : head + 1] * fade + jnp.sum(weights, axis=0, keepdims=True)
        rows = slice(head * HEAD_DIM, (head + 1) * HEAD_DIM)
        part = dot(values, weights.astype(BF16), TN)
        acc[rows] = acc[rows] * fade + part[rows]

    @pl.when(step == pl.num_programs(0) - 1)
    def _():
        scale = 1.0 / total[:heads]
        parts = [
            acc[head * HEAD_DIM : (head + 1) * HEAD_DIM] * scale[head : head + 1] for head in range(heads)
        ]
        out_ref[...] = jnp.concatenate(parts, axis=0).T
        lse_ref[...] = top[...] + jnp.log(jnp.maximum(total[...], 1e-30))


def attention_backward_kernel(
    q_ref, kv_ref, qid_ref, mark_ref, out_ref, lse_ref, do_ref, dq_ref, dkv_ref, qm, dom, acc, delta
):
    step = pl.program_id(0)
    heads = qm.shape[0]
    width = q_ref.shape[1]

    @pl.when(step == 0)
    def _():
        scaled = q_ref[...] * jnp.asarray(0.125, BF16)
        incoming = do_ref[...]
        for head in range(heads):
            qm[head] = head_lanes(scaled, head)
            dom[head] = head_lanes(incoming, head)
        product = incoming.astype(F32) * out_ref[...]
        row = lax.broadcasted_iota(jnp.int32, (8, width), 0)
        lane = lax.broadcasted_iota(jnp.int32, (8, width), 1)
        chooser = jnp.where(lane // HEAD_DIM == row, 1.0, 0.0).astype(F32)
        delta[...] = lax.dot_general(
            chooser, product, NT, preferred_element_type=F32, precision=lax.Precision.HIGHEST
        )
        acc[...] = jnp.zeros_like(acc)

    keys = kv_ref[:, :width]
    values = kv_ref[:, width:]
    allowed = mark_ref[...] == qid_ref[...]
    grad_keys = jnp.zeros(keys.shape, F32)
    grad_values = jnp.zeros(keys.shape, F32)
    for head in range(heads):
        scores = dot(keys, qm[head], NT)
        weights = jnp.where(allowed, jnp.exp(scores - lse_ref[head : head + 1]), 0.0)
        grad_weights = dot(values, dom[head], NT)
        grad_scores = (weights * (grad_weights - delta[head : head + 1])).astype(BF16)
        grad_values += dot(weights.astype(BF16), dom[head])
        grad_keys += dot(grad_scores, qm[head])
        rows = slice(head * HEAD_DIM, (head + 1) * HEAD_DIM)
        acc[rows] += dot(keys, grad_scores, TN)[rows]
    dkv_ref[:, :width] = grad_keys.astype(BF16)
    dkv_ref[:, width:] = grad_values.astype(BF16)

    @pl.when(step == pl.num_programs(0) - 1)
    def _():
        dq_ref[...] = (acc[...] * 0.125).T.astype(BF16)


def key_block(count):
    return 256 if count % 256 == 0 else count


def whole(shape):
    return pl.BlockSpec(shape, lambda step: (0,) * len(shape))


def attention_cost(rows, count, width, products):
    return pl.CostEstimate(
        flops=16 * products * 2 * rows * count * width,
        bytes_accessed=rows * width * 12 + count * width * 8,
        transcendentals=rows * count * (width // HEAD_DIM),
    )


def attention_forward(queries, pairs, query_ids, marks):
    rows, width = queries.shape
    count = pairs.shape[0]
    heads = width // HEAD_DIM
    block = key_block(count)
    return pl.pallas_call(
        attention_forward_kernel,
        grid=(count // block,),
        in_specs=[
            whole((rows, width)),
            pl.BlockSpec((block, 2 * width), lambda step: (step, 0)),
            whole((1, rows)),
            pl.BlockSpec((block, 1), lambda step: (step, 0)),
        ],
        out_specs=[whole((rows, width)), whole((8, rows))],
        out_shape=[
            jax.ShapeDtypeStruct((rows, width), F32),
            jax.ShapeDtypeStruct((8, rows), F32),
        ],
        scratch_shapes=[
            pltpu.VMEM((heads, rows, width), BF16),
            pltpu.VMEM((width, rows), F32),
            pltpu.VMEM((8, rows), F32),
            pltpu.VMEM((8, rows), F32),
        ],
        compiler_params=pltpu.CompilerParams(vmem_limit_bytes=VMEM_LIMIT),
        cost_estimate=attention_cost(rows, count, width, 2),
        name="attention_forward",
    )(queries, pairs, query_ids, marks)


def attention_backward(queries, pairs, query_ids, marks, out, lse, grad_out):
    rows, width = queries.shape
    count = pairs.shape[0]
    heads = width // HEAD_DIM
    block = key_block(count)
    return pl.pallas_call(
        attention_backward_kernel,
        grid=(count // block,),
        in_specs=[
            whole((rows, width)),
            pl.BlockSpec((block, 2 * width), lambda step: (step, 0)),
            whole((1, rows)),
            pl.BlockSpec((block, 1), lambda step: (step, 0)),
            whole((rows, width)),
            whole((8, rows)),
            whole((rows, width)),
        ],
        out_specs=[
            whole((rows, width)),
            pl.BlockSpec((block, 2 * width), lambda step: (step, 0)),
        ],
        out_shape=[
            jax.ShapeDtypeStruct((rows, width), BF16),
            jax.ShapeDtypeStruct((count, 2 * width), BF16),
        ],
        scratch_shapes=[
            pltpu.VMEM((heads, rows, width), BF16),
            pltpu.VMEM((heads, rows, width), BF16),
            pltpu.VMEM((width, rows), F32),
            pltpu.VMEM((8, rows), F32),
        ],
        compiler_params=pltpu.CompilerParams(vmem_limit_bytes=VMEM_LIMIT),
        cost_estimate=attention_cost(rows, count, width, 5),
        name="attention_backward",
    )(queries, pairs, query_ids, marks, out, lse, grad_out)


def norm_forward(value, gain, shift):
    centre = value - jnp.mean(value, axis=-1, keepdims=True)
    inverse = lax.rsqrt(jnp.mean(centre * centre, axis=-1, keepdims=True) + 1e-05)
    unit = centre * inverse
    return unit * gain + shift, unit, inverse


def norm_backward(grad, unit, inverse, gain):
    scaled = grad * gain
    mean_one = jnp.mean(scaled, axis=-1, keepdims=True)
    mean_two = jnp.mean(scaled * unit, axis=-1, keepdims=True)
    return (
        inverse * (scaled - mean_one - unit * mean_two),
        jnp.sum(grad * unit, axis=0),
        jnp.sum(grad, axis=0),
    )


def body(
    tokens,
    cotangent,
    doc_ids,
    pad_mask,
    w_query,
    w_key,
    w_value,
    w_out,
    b_query,
    b_value,
    b_out,
    gain_attn,
    bias_attn,
    w_up,
    b_up,
    w_down,
    b_down,
    gain_ffn,
    bias_ffn,
):
    section = lax.axis_index("section")
    head_count = lax.axis_size("head")
    blk_count = lax.axis_size("blk")
    head_at = lax.axis_index("head")
    blk_at = lax.axis_index("blk")
    batches, rows, width = tokens.shape
    shard = width // (head_count * blk_count)
    hidden_width = w_up.shape[2]
    chunks = hidden_width // width
    half = blk_count // 2
    middles = blk_count // 4
    per_section = batches // 2
    members = 4
    part_width = width // members
    pair_width = 2 * part_width
    first_section = section == 0
    low_half = blk_at < half
    member = (head_at // 2) * 2 + blk_at % 2
    own_batch = section * per_section + blk_at // half
    other_batch = section * per_section + 1 - blk_at // half

    def across_section(value):
        return lax.ppermute(value, "section", [(0, 1), (1, 0)])

    def across_half(value):
        return lax.ppermute(value, "blk", [(at, (at + half) % blk_count) for at in range(blk_count)])

    def across_member(value, step):
        pairs = []
        for head in range(head_count):
            for blk in range(blk_count):
                there = (head ^ (step & 2)) * blk_count + (blk ^ (step & 1))
                pairs.append((head * blk_count + blk, there))
        return lax.ppermute(value, GROUP, pairs)

    def across_core(value):
        return lax.ppermute(value, "head", [(at, at ^ 1) for at in range(head_count)])

    def across_middle(value, step):
        pairs = []
        for at in range(blk_count):
            base, middle, low = at // half, (at % half) // 2, at % 2
            pairs.append((at, base * half + ((middle + step) % middles) * 2 + low))
        return lax.ppermute(value, "blk", pairs)

    direct = head_count == 4 and blk_count == 4
    core_at = head_at % 2
    side_at = head_at // 2

    def across_side(value):
        return lax.ppermute(value, "head", [(at, at ^ 2) for at in range(head_count)])

    def add(*values):
        return sum(value.astype(F32) for value in values).astype(BF16)

    def tied(*values):
        return lax.optimization_barrier(values)

    def halves(value, axis):
        shape = value.shape
        lead = shape[axis] // width
        split = value.reshape(shape[:axis] + (lead, 2, 2, width // 4) + shape[axis + 1 :])
        first = lax.index_in_dim(split, 0, axis + 2, keepdims=False)
        second = lax.index_in_dim(split, 1, axis + 2, keepdims=False)
        flat = shape[:axis] + (shape[axis] // 2,) + shape[axis + 1 :]
        return (
            jnp.where(core_at == 0, first, second).reshape(flat),
            jnp.where(core_at == 0, second, first).reshape(flat),
        )

    def weight_grad(left, right):
        return [dot(part, right, TN).astype(BF16) for part in halves(left, 1)]

    def chip_parts(parts):
        return [parts[0], across_core(parts[1])]

    def side_sum(parts):
        views = [part.reshape(-1, 2, blk_count, shard, part.shape[1]) for part in parts]

        def at(which):
            return [lax.dynamic_index_in_dim(view, which, 1, keepdims=False) for view in views]

        return add(*at(side_at), across_side(add(*at(1 - side_at))))

    def line_sum(value):
        return lax.psum_scatter(value, "blk", scatter_dimension=0, tiled=True)[0]

    def pick(value, at):
        return lax.dynamic_index_in_dim(value, at, 0, keepdims=False)

    def to_heads(groups):
        own = [pick(groups, member ^ step) for step in range(members)]
        return jnp.concatenate(
            [own[0]] + [across_member(own[step], step) for step in range(1, members)], axis=0
        )

    def to_tokens(value):
        parts = value.reshape(members, value.shape[0] // members, value.shape[1])
        back = jnp.stack(
            [parts[0]] + [across_member(parts[step], step) for step in range(1, members)], axis=0
        )
        return [pick(back, member ^ at) for at in range(members)]

    def all_keys(value):
        value = jnp.concatenate([value, across_core(value)], axis=0)
        return jnp.concatenate(
            [value] + [across_middle(value, step) for step in range(1, middles)], axis=0
        )

    def own_keys_sum(value):
        count = value.shape[0] // middles
        total = value[:count].astype(F32)
        for step in range(1, middles):
            back = across_middle(value[step * count : (step + 1) * count], middles - step)
            total = total + back.astype(F32)
        partner = across_core(total[count // 2 :].astype(BF16))
        return (total[: count // 2] + partner.astype(F32)).astype(BF16)

    def columns(value, size):
        return value.reshape(value.shape[0], members, size).transpose(1, 0, 2)

    def split_parts(value):
        return value[0].reshape(shard, members, part_width)

    pairs_local = jnp.concatenate([split_parts(w_key), split_parts(w_value)], axis=2)
    small_local = jnp.stack(
        [
            part.reshape(shard)
            for part in (b_query, b_value, b_out, gain_attn, bias_attn, b_down, gain_ffn, bias_ffn)
        ]
        + [b_up[0].reshape(chunks, shard)[at] for at in range(chunks)],
        axis=1,
    )
    small_count = small_local.shape[1]
    joint_width = 3 * width
    first_local = jnp.concatenate(
        [
            pairs_local.reshape(shard, 2 * width),
            w_query[0],
            jnp.pad(small_local, ((0, 0), (0, 128 - small_count))),
        ],
        axis=1,
    )
    up_local = (
        w_up[0]
        .reshape(shard, head_count * blk_count, chunks, shard)
        .transpose(0, 2, 1, 3)
        .reshape(shard, hidden_width)
    )
    down_local = jnp.concatenate(
        [w_down[0, at * shard : (at + 1) * shard] for at in range(chunks)], axis=1
    )
    rest_local = jnp.concatenate([w_out[0], up_local, down_local], axis=1)
    rest_other = across_section(rest_local)
    first_all = lax.all_gather(first_local, ("section",) + GROUP, axis=0, tiled=True)
    rest_all = [
        lax.all_gather(
            jnp.where(first_section, rest_local, rest_other), GROUP, axis=0, tiled=True
        ),
        lax.all_gather(
            jnp.where(first_section, rest_other, rest_local), GROUP, axis=0, tiled=True
        ),
    ]

    def both_blocks(value):
        return jnp.concatenate(
            [pick(value, own_batch), across_half(pick(value, other_batch))], axis=0
        )

    layer_in = both_blocks(tokens)
    grad_top = both_blocks(cotangent)
    marks_local = jnp.where(pad_mask == 1, doc_ids, -1)
    labels = both_blocks(jnp.stack([doc_ids, marks_local], axis=-1))
    labels = jnp.concatenate(
        [labels] + [across_member(labels, step) for step in range(1, members)], axis=0
    )
    query_ids = labels[:, 0].reshape(1, -1)
    key_marks = all_keys(labels)[:, 1].reshape(-1, 1)

    layers = []
    outputs = []
    for layer in range(2):
        joint = first_all[layer * width : (layer + 1) * width, :joint_width]
        small = first_all[layer * width : (layer + 1) * width, joint_width:].T.astype(F32)
        rest = rest_all[layer]
        out_weight = rest[:, :width]
        up_weight = rest[:, width : width + hidden_width]
        down_weight = [
            rest[:, width + hidden_width + at * width : width + hidden_width + (at + 1) * width]
            for at in range(chunks)
        ]
        q_shift, v_shift, out_shift, gain_one, shift_one, down_shift, gain_two, shift_two = [
            small[at] for at in range(8)
        ]
        up_shift = small[8 : 8 + chunks].reshape(hidden_width)
        pair_shift = jnp.concatenate(
            [jnp.zeros((members, part_width), F32), v_shift.reshape(members, part_width)], axis=1
        )
        joint_shift = jnp.concatenate([pair_shift.reshape(2 * width), q_shift])
        joint_rows = (dot(layer_in, joint) + joint_shift).astype(BF16)
        pairs = all_keys(to_heads(columns(joint_rows[:, : 2 * width], pair_width)))
        queries = to_heads(columns(joint_rows[:, 2 * width :], part_width))
        mixed, lse = attention_forward(queries, pairs, query_ids, key_marks)
        attended = jnp.concatenate(to_tokens(mixed.astype(BF16)), axis=1)
        first_sum = layer_in.astype(F32) + dot(attended, out_weight) + out_shift
        middle, unit_one, inverse_one = norm_forward(first_sum, gain_one, shift_one)
        middle_low = middle.astype(BF16)
        hidden = dot(middle_low, up_weight) + up_shift
        share = 0.5 * lax.erfc(hidden * (-(0.5**0.5)))
        slope = share + hidden * jnp.exp(hidden * hidden * -0.5) * 0.3989422804014327
        active = (hidden * share).astype(BF16)
        second = middle + down_shift
        for at in range(chunks):
            second = second + dot(active[:, at * width : (at + 1) * width], down_weight[at])
        result, unit_two, inverse_two = norm_forward(second, gain_two, shift_two)
        layers.append(
            (
                layer_in,
                joint,
                out_weight,
                up_weight,
                down_weight,
                gain_one,
                gain_two,
                pairs,
                queries,
                mixed,
                lse,
                attended,
                unit_one,
                inverse_one,
                middle_low,
                slope,
                active,
                unit_two,
                inverse_two,
            )
        )
        layer_in = result.astype(BF16)
        outputs.append(layer_in)

    def reduced(value):
        return lax.psum_scatter(value, GROUP, scatter_dimension=0, tiled=True)

    wide_sums = [None, None]
    last_sums = [None, None]
    grads = [None, None]
    for layer in (1, 0):
        (
            layer_in,
            joint,
            out_weight,
            up_weight,
            down_weight,
            gain_one,
            gain_two,
            pairs,
            queries,
            mixed,
            lse,
            attended,
            unit_one,
            inverse_one,
            middle_low,
            slope,
            active,
            unit_two,
            inverse_two,
        ) = layers[layer]
        grad_second, grad_gain_two, grad_shift_two = norm_backward(
            grad_top, unit_two, inverse_two, gain_two
        )
        grad_down_low = grad_second.astype(BF16)
        grad_active = jnp.concatenate(
            [dot(grad_down_low, down_weight[at], NT) for at in range(chunks)], axis=1
        )
        grad_hidden = (grad_active * slope).astype(BF16)
        grad_down = [
            dot(active[:, at * width : (at + 1) * width], grad_down_low, TN).astype(BF16)
            for at in range(chunks)
        ]
        grad_up = dot(middle_low, grad_hidden, TN).astype(BF16)
        parts = [grad_up] + grad_down + ([last] if layer == 0 else [])
        grad_hidden, wide = tied(grad_hidden, jnp.concatenate(parts, axis=1))
        if layer == 0:
            wide, wide_sums[1] = tied(wide, wide_sums[1])
        wide_sums[layer] = reduced(wide)
        grad_middle = grad_second + dot(grad_hidden, up_weight, NT)
        grad_first, grad_gain_one, grad_shift_one = norm_backward(
            grad_middle, unit_one, inverse_one, gain_one
        )
        grad_branch = grad_first.astype(BF16)
        grad_returned = dot(grad_branch, out_weight, NT).astype(BF16)
        grad_mixed = to_heads(columns(grad_returned, part_width))
        grad_queries, grad_pairs = attention_backward(
            queries, pairs, query_ids, key_marks, mixed, lse, grad_mixed
        )
        pair_parts = to_tokens(own_keys_sum(grad_pairs))
        query_parts = to_tokens(grad_queries)
        grad_joint = jnp.concatenate(pair_parts + query_parts, axis=1)
        grad_input = grad_first + dot(grad_joint, joint, NT)
        joint_sum = jnp.sum(grad_joint.astype(F32), axis=0)
        small = jnp.stack(
            [
                joint_sum[2 * width :],
                joint_sum[: 2 * width].reshape(members, 2, part_width)[:, 1].reshape(width),
                jnp.sum(grad_branch.astype(F32), axis=0),
                grad_gain_one,
                grad_shift_one,
                jnp.sum(grad_down_low.astype(F32), axis=0),
                grad_gain_two,
                grad_shift_two,
            ],
            axis=0,
        )
        hidden_sum = jnp.sum(grad_hidden.astype(F32), axis=0).reshape(chunks, width)
        small = jnp.concatenate([small, hidden_sum], axis=0).astype(BF16)
        small = jnp.pad(small.T, ((0, 0), (0, 128 - small_count)))
        if direct and layer == 0:
            last_side = side_sum(
                chip_parts(
                    [
                        jnp.concatenate(group, axis=1)
                        for group in zip(
                            weight_grad(layer_in, grad_joint),
                            weight_grad(attended, grad_branch),
                            halves(small, 0),
                        )
                    ]
                )
            )[0]
        else:
            last = jnp.concatenate(
                [
                    dot(layer_in, grad_joint, TN).astype(BF16),
                    dot(attended, grad_branch, TN).astype(BF16),
                    small,
                ],
                axis=1,
            )
        grads[layer] = grad_input
        grad_top = grad_input.astype(BF16).astype(F32)

    def settle(first, second):
        to_first = lax.ppermute(first, "section", [(1, 0)])
        to_second = lax.ppermute(second, "section", [(0, 1)])
        return jnp.where(first_section, first, second).astype(F32) + jnp.where(
            first_section, to_first, to_second
        ).astype(F32)

    if direct:
        last_side, wide_sums[0] = tied(last_side, wide_sums[0])
        last_sums[0] = line_sum(last_side)
    else:
        last_sums[0] = reduced(last)
    last_sums[1] = wide_sums[0][:, 2 * hidden_width :]
    wide_sums[0] = wide_sums[0][:, : 2 * hidden_width]
    wide = settle(wide_sums[0], wide_sums[1])
    last = settle(last_sums[0], last_sums[1])
    grad_up = (
        wide[:, :hidden_width]
        .reshape(shard, chunks, head_count * blk_count, shard)
        .transpose(0, 2, 1, 3)
        .reshape(shard, hidden_width)
    )
    grad_down = jnp.concatenate(
        [
            wide[:, hidden_width + at * width : hidden_width + (at + 1) * width]
            for at in range(chunks)
        ],
        axis=0,
    )
    grad_pairs = last[:, : 2 * width].reshape(shard, members, 2, part_width)
    grad_key = grad_pairs[:, :, 0].reshape(shard, width)
    grad_value = grad_pairs[:, :, 1].reshape(shard, width)
    grad_query = last[:, 2 * width : 3 * width]
    grad_out = last[:, 3 * width : 4 * width]
    small = last[:, 4 * width :].T

    def placed_rows(first, second):
        def halves(value):
            got = across_half(value[rows:])
            own = value[:rows]
            return jnp.stack([jnp.where(low_half, own, got), jnp.where(low_half, got, own)], axis=0)

        first, second = halves(first), halves(second)
        got = across_section(jnp.where(first_section, second, first))
        kept = jnp.where(first_section, first, second)
        return jnp.where(
            first_section,
            jnp.concatenate([kept, got], axis=0),
            jnp.concatenate([got, kept], axis=0),
        )

    outputs_all = placed_rows(outputs[0], outputs[1])
    grad_inputs = placed_rows(grads[0], grads[1])
    return (
        outputs_all[None],
        grad_inputs[None],
        grad_query[None],
        grad_key[None],
        grad_value[None],
        grad_out[None],
        small[0][None],
        small[1][None],
        small[2][None],
        small[3][None],
        small[4][None],
        grad_up[None],
        small[8 : 8 + chunks].reshape(1, chunks * shard),
        grad_down[None],
        small[5][None],
        small[6][None],
        small[7][None],
    )


def solution(mesh):
    rows = P(None, GROUP, None)
    marks = P(None, GROUP)
    matrix = P("section", GROUP, None)
    vector = P("section", GROUP)
    result = P("section", None, GROUP, None)
    return jax.shard_map(
        body,
        mesh=mesh,
        in_specs=(rows, rows, marks, marks)
        + (matrix,) * 4
        + (vector,) * 5
        + (matrix, vector, matrix, vector, vector, vector),
        out_specs=(result, result)
        + (matrix,) * 4
        + (vector,) * 5
        + (matrix, vector, matrix, vector, vector, vector),
        check_vma=False,
    )
```

```python
import functools

import jax
import jax.numpy as jnp
from jax import lax
from jax.experimental import pallas as pl
from jax.experimental.pallas import tpu as pltpu
from jax.sharding import PartitionSpec as P

HEAD_DIM = 64
GROUP = ("head", "blk")
F32 = jnp.float32
BF16 = jnp.bfloat16
NT = (((1,), (1,)), ((), ()))
NN = (((1,), (0,)), ((), ()))
TN = (((0,), (0,)), ((), ()))
VMEM_LIMIT = 48 * 1024 * 1024


def dot(left, right, dims=NN):
    return lax.dot_general(left, right, dims, preferred_element_type=F32)


def head_lanes(value, head):
    lane = lax.broadcasted_iota(jnp.int32, value.shape, 1)
    return jnp.where(lane // HEAD_DIM == head, value, jnp.zeros_like(value))


def attention_forward_kernel(q_ref, kv_ref, qid_ref, mark_ref, out_ref, lse_ref, qm, acc, top, total):
    step = pl.program_id(0)
    heads = qm.shape[0]
    width = q_ref.shape[1]

    @pl.when(step == 0)
    def _():
        scaled = q_ref[...] * jnp.asarray(0.125, BF16)
        for head in range(heads):
            qm[head] = head_lanes(scaled, head)
        acc[...] = jnp.zeros_like(acc)
        top[...] = jnp.full_like(top, -1e30)
        total[...] = jnp.zeros_like(total)

    keys = kv_ref[:, :width]
    values = kv_ref[:, width:]
    allowed = mark_ref[...] == qid_ref[...]
    for head in range(heads):
        scores = jnp.where(allowed, dot(keys, qm[head], NT), -1e30)
        before = top[head : head + 1]
        after = jnp.maximum(before, jnp.max(scores, axis=0, keepdims=True))
        weights = jnp.exp(scores - after)
        fade = jnp.exp(before - after)
        top[head : head + 1] = after
        total[head : head + 1] = total[head : head + 1] * fade + jnp.sum(weights, axis=0, keepdims=True)
        rows = slice(head * HEAD_DIM, (head + 1) * HEAD_DIM)
        part = dot(values, weights.astype(BF16), TN)
        acc[rows] = acc[rows] * fade + part[rows]

    @pl.when(step == pl.num_programs(0) - 1)
    def _():
        scale = 1.0 / total[:heads]
        parts = [
            acc[head * HEAD_DIM : (head + 1) * HEAD_DIM] * scale[head : head + 1] for head in range(heads)
        ]
        out_ref[...] = jnp.concatenate(parts, axis=0).T
        lse_ref[...] = top[...] + jnp.log(jnp.maximum(total[...], 1e-30))


def attention_backward_kernel(
    q_ref, kv_ref, qid_ref, mark_ref, out_ref, lse_ref, do_ref, dq_ref, dkv_ref, qm, dom, acc, delta
):
    step = pl.program_id(0)
    heads = qm.shape[0]
    width = q_ref.shape[1]

    @pl.when(step == 0)
    def _():
        scaled = q_ref[...] * jnp.asarray(0.125, BF16)
        incoming = do_ref[...]
        for head in range(heads):
            qm[head] = head_lanes(scaled, head)
            dom[head] = head_lanes(incoming, head)
        product = incoming.astype(F32) * out_ref[...]
        row = lax.broadcasted_iota(jnp.int32, (8, width), 0)
        lane = lax.broadcasted_iota(jnp.int32, (8, width), 1)
        chooser = jnp.where(lane // HEAD_DIM == row, 1.0, 0.0).astype(F32)
        delta[...] = lax.dot_general(
            chooser, product, NT, preferred_element_type=F32, precision=lax.Precision.HIGHEST
        )
        acc[...] = jnp.zeros_like(acc)

    keys = kv_ref[:, :width]
    values = kv_ref[:, width:]
    allowed = mark_ref[...] == qid_ref[...]
    grad_keys = jnp.zeros(keys.shape, F32)
    grad_values = jnp.zeros(keys.shape, F32)
    for head in range(heads):
        scores = dot(keys, qm[head], NT)
        weights = jnp.where(allowed, jnp.exp(scores - lse_ref[head : head + 1]), 0.0)
        grad_weights = dot(values, dom[head], NT)
        grad_scores = (weights * (grad_weights - delta[head : head + 1])).astype(BF16)
        grad_values += dot(weights.astype(BF16), dom[head])
        grad_keys += dot(grad_scores, qm[head])
        rows = slice(head * HEAD_DIM, (head + 1) * HEAD_DIM)
        acc[rows] += dot(keys, grad_scores, TN)[rows]
    dkv_ref[:, :width] = grad_keys.astype(BF16)
    dkv_ref[:, width:] = grad_values.astype(BF16)

    @pl.when(step == pl.num_programs(0) - 1)
    def _():
        dq_ref[...] = (acc[...] * 0.125).T.astype(BF16)


def key_block(count):
    return 256 if count % 256 == 0 else count


def whole(shape):
    return pl.BlockSpec(shape, lambda step: (0,) * len(shape))


def attention_cost(rows, count, width, products):
    return pl.CostEstimate(
        flops=16 * products * 2 * rows * count * width,
        bytes_accessed=rows * width * 12 + count * width * 8,
        transcendentals=rows * count * (width // HEAD_DIM),
    )


def attention_forward(queries, pairs, query_ids, marks):
    rows, width = queries.shape
    count = pairs.shape[0]
    heads = width // HEAD_DIM
    block = key_block(count)
    return pl.pallas_call(
        attention_forward_kernel,
        grid=(count // block,),
        in_specs=[
            whole((rows, width)),
            pl.BlockSpec((block, 2 * width), lambda step: (step, 0)),
            whole((1, rows)),
            pl.BlockSpec((block, 1), lambda step: (step, 0)),
        ],
        out_specs=[whole((rows, width)), whole((8, rows))],
        out_shape=[
            jax.ShapeDtypeStruct((rows, width), F32),
            jax.ShapeDtypeStruct((8, rows), F32),
        ],
        scratch_shapes=[
            pltpu.VMEM((heads, rows, width), BF16),
            pltpu.VMEM((width, rows), F32),
            pltpu.VMEM((8, rows), F32),
            pltpu.VMEM((8, rows), F32),
        ],
        compiler_params=pltpu.CompilerParams(vmem_limit_bytes=VMEM_LIMIT),
        cost_estimate=attention_cost(rows, count, width, 2),
        name="attention_forward",
    )(queries, pairs, query_ids, marks)


def attention_backward(queries, pairs, query_ids, marks, out, lse, grad_out):
    rows, width = queries.shape
    count = pairs.shape[0]
    heads = width // HEAD_DIM
    block = key_block(count)
    return pl.pallas_call(
        attention_backward_kernel,
        grid=(count // block,),
        in_specs=[
            whole((rows, width)),
            pl.BlockSpec((block, 2 * width), lambda step: (step, 0)),
            whole((1, rows)),
            pl.BlockSpec((block, 1), lambda step: (step, 0)),
            whole((rows, width)),
            whole((8, rows)),
            whole((rows, width)),
        ],
        out_specs=[
            whole((rows, width)),
            pl.BlockSpec((block, 2 * width), lambda step: (step, 0)),
        ],
        out_shape=[
            jax.ShapeDtypeStruct((rows, width), BF16),
            jax.ShapeDtypeStruct((count, 2 * width), BF16),
        ],
        scratch_shapes=[
            pltpu.VMEM((heads, rows, width), BF16),
            pltpu.VMEM((heads, rows, width), BF16),
            pltpu.VMEM((width, rows), F32),
            pltpu.VMEM((8, rows), F32),
        ],
        compiler_params=pltpu.CompilerParams(vmem_limit_bytes=VMEM_LIMIT),
        cost_estimate=attention_cost(rows, count, width, 5),
        name="attention_backward",
    )(queries, pairs, query_ids, marks, out, lse, grad_out)


def norm_forward(value, gain, shift):
    centre = value - jnp.mean(value, axis=-1, keepdims=True)
    inverse = lax.rsqrt(jnp.mean(centre * centre, axis=-1, keepdims=True) + 1e-05)
    unit = centre * inverse
    return unit * gain + shift, unit, inverse


def norm_backward(grad, unit, inverse, gain):
    scaled = grad * gain
    mean_one = jnp.mean(scaled, axis=-1, keepdims=True)
    mean_two = jnp.mean(scaled * unit, axis=-1, keepdims=True)
    return (
        inverse * (scaled - mean_one - unit * mean_two),
        jnp.sum(grad * unit, axis=0),
        jnp.sum(grad, axis=0),
    )


def body(
    tokens,
    cotangent,
    doc_ids,
    pad_mask,
    w_query,
    w_key,
    w_value,
    w_out,
    b_query,
    b_value,
    b_out,
    gain_attn,
    bias_attn,
    w_up,
    b_up,
    w_down,
    b_down,
    gain_ffn,
    bias_ffn,
):
    section = lax.axis_index("section")
    head_count = lax.axis_size("head")
    blk_count = lax.axis_size("blk")
    head_at = lax.axis_index("head")
    blk_at = lax.axis_index("blk")
    batches, rows, width = tokens.shape
    shard = width // (head_count * blk_count)
    hidden_width = w_up.shape[2]
    chunks = hidden_width // width
    half = blk_count // 2
    middles = blk_count // 4
    per_section = batches // 2
    members = 4
    part_width = width // members
    pair_width = 2 * part_width
    first_section = section == 0
    low_half = blk_at < half
    member = (head_at // 2) * 2 + blk_at % 2
    own_batch = section * per_section + blk_at // half
    other_batch = section * per_section + 1 - blk_at // half

    def across_section(value):
        return lax.ppermute(value, "section", [(0, 1), (1, 0)])

    def across_half(value):
        return lax.ppermute(value, "blk", [(at, (at + half) % blk_count) for at in range(blk_count)])

    def across_member(value, step):
        pairs = []
        for head in range(head_count):
            for blk in range(blk_count):
                there = (head ^ (step & 2)) * blk_count + (blk ^ (step & 1))
                pairs.append((head * blk_count + blk, there))
        return lax.ppermute(value, GROUP, pairs)

    def across_core(value):
        return lax.ppermute(value, "head", [(at, at ^ 1) for at in range(head_count)])

    def across_middle(value, step):
        pairs = []
        for at in range(blk_count):
            base, middle, low = at // half, (at % half) // 2, at % 2
            pairs.append((at, base * half + ((middle + step) % middles) * 2 + low))
        return lax.ppermute(value, "blk", pairs)

    direct = head_count == 4 and blk_count == 4
    core_at = head_at % 2
    side_at = head_at // 2

    def across_side(value):
        return lax.ppermute(value, "head", [(at, at ^ 2) for at in range(head_count)])

    def add(*values):
        return sum(value.astype(F32) for value in values).astype(BF16)

    def tied(*values):
        return lax.optimization_barrier(values)

    def halves(value, axis):
        shape = value.shape
        lead = shape[axis] // width
        split = value.reshape(shape[:axis] + (lead, 2, 2, width // 4) + shape[axis + 1 :])
        first = lax.index_in_dim(split, 0, axis + 2, keepdims=False)
        second = lax.index_in_dim(split, 1, axis + 2, keepdims=False)
        flat = shape[:axis] + (shape[axis] // 2,) + shape[axis + 1 :]
        return (
            jnp.where(core_at == 0, first, second).reshape(flat),
            jnp.where(core_at == 0, second, first).reshape(flat),
        )

    def weight_grad(left, right):
        return [dot(part, right, TN).astype(BF16) for part in halves(left, 1)]

    def chip_parts(parts):
        return [parts[0], across_core(parts[1])]

    def side_sum(parts):
        views = [part.reshape(-1, 2, blk_count, shard, part.shape[1]) for part in parts]

        def at(which):
            return [lax.dynamic_index_in_dim(view, which, 1, keepdims=False) for view in views]

        return add(*at(side_at), across_side(add(*at(1 - side_at))))

    def line_sum(value):
        return lax.psum_scatter(value, "blk", scatter_dimension=0, tiled=True)[0]

    def pick(value, at):
        return lax.dynamic_index_in_dim(value, at, 0, keepdims=False)

    def to_heads(groups):
        own = [pick(groups, member ^ step) for step in range(members)]
        return jnp.concatenate(
            [own[0]] + [across_member(own[step], step) for step in range(1, members)], axis=0
        )

    def to_tokens(value):
        parts = value.reshape(members, value.shape[0] // members, value.shape[1])
        back = jnp.stack(
            [parts[0]] + [across_member(parts[step], step) for step in range(1, members)], axis=0
        )
        return [pick(back, member ^ at) for at in range(members)]

    def all_keys(value):
        value = jnp.concatenate([value, across_core(value)], axis=0)
        return jnp.concatenate(
            [value] + [across_middle(value, step) for step in range(1, middles)], axis=0
        )

    def own_keys_sum(value):
        count = value.shape[0] // middles
        total = value[:count].astype(F32)
        for step in range(1, middles):
            back = across_middle(value[step * count : (step + 1) * count], middles - step)
            total = total + back.astype(F32)
        partner = across_core(total[count // 2 :].astype(BF16))
        return (total[: count // 2] + partner.astype(F32)).astype(BF16)

    def columns(value, size):
        return value.reshape(value.shape[0], members, size).transpose(1, 0, 2)

    def split_parts(value):
        return value[0].reshape(shard, members, part_width)

    joint_local = jnp.concatenate(
        [split_parts(w_key), split_parts(w_value), split_parts(w_query)], axis=2
    )
    small_local = jnp.stack(
        [
            part.reshape(shard)
            for part in (b_query, b_value, b_out, gain_attn, bias_attn, b_down, gain_ffn, bias_ffn)
        ]
        + [b_up[0].reshape(chunks, shard)[at] for at in range(chunks)],
        axis=1,
    )
    small_count = small_local.shape[1]
    joint_width = 3 * width
    first_local = jnp.concatenate(
        [
            joint_local.reshape(shard, joint_width),
            jnp.pad(small_local, ((0, 0), (0, 128 - small_count))),
        ],
        axis=1,
    )
    up_local = (
        w_up[0]
        .reshape(shard, head_count * blk_count, chunks, shard)
        .transpose(0, 2, 1, 3)
        .reshape(shard, hidden_width)
    )
    down_local = jnp.concatenate(
        [w_down[0, at * shard : (at + 1) * shard] for at in range(chunks)], axis=1
    )
    rest_local = jnp.concatenate([w_out[0], up_local, down_local], axis=1)
    rest_other = across_section(rest_local)
    first_all = lax.all_gather(first_local, ("section",) + GROUP, axis=0, tiled=True)
    rest_all = [
        lax.all_gather(
            jnp.where(first_section, rest_local, rest_other), GROUP, axis=0, tiled=True
        ),
        lax.all_gather(
            jnp.where(first_section, rest_other, rest_local), GROUP, axis=0, tiled=True
        ),
    ]

    def both_blocks(value):
        return jnp.concatenate(
            [pick(value, own_batch), across_half(pick(value, other_batch))], axis=0
        )

    layer_in = both_blocks(tokens)
    grad_top = both_blocks(cotangent)
    marks_local = jnp.where(pad_mask == 1, doc_ids, -1)
    labels = both_blocks(jnp.stack([doc_ids, marks_local], axis=-1))
    labels = jnp.concatenate(
        [labels] + [across_member(labels, step) for step in range(1, members)], axis=0
    )
    query_ids = labels[:, 0].reshape(1, -1)
    key_marks = all_keys(labels)[:, 1].reshape(-1, 1)

    layers = []
    outputs = []
    for layer in range(2):
        joint = first_all[layer * width : (layer + 1) * width, :joint_width]
        small = first_all[layer * width : (layer + 1) * width, joint_width:].T.astype(F32)
        rest = rest_all[layer]
        out_weight = rest[:, :width]
        up_weight = rest[:, width : width + hidden_width]
        down_weight = [
            rest[:, width + hidden_width + at * width : width + hidden_width + (at + 1) * width]
            for at in range(chunks)
        ]
        q_shift, v_shift, out_shift, gain_one, shift_one, down_shift, gain_two, shift_two = [
            small[at] for at in range(8)
        ]
        up_shift = small[8 : 8 + chunks].reshape(hidden_width)
        joint_shift = jnp.concatenate(
            [
                jnp.zeros((members, part_width), F32),
                v_shift.reshape(members, part_width),
                q_shift.reshape(members, part_width),
            ],
            axis=1,
        )
        joint_rows = (dot(layer_in, joint) + joint_shift.reshape(joint_width)).astype(BF16)
        arrived = to_heads(columns(joint_rows, pair_width + part_width))
        pairs = all_keys(arrived[:, :pair_width])
        queries = arrived[:, pair_width:]
        mixed, lse = attention_forward(queries, pairs, query_ids, key_marks)
        attended = jnp.concatenate(to_tokens(mixed.astype(BF16)), axis=1)
        first_sum = layer_in.astype(F32) + dot(attended, out_weight) + out_shift
        middle, unit_one, inverse_one = norm_forward(first_sum, gain_one, shift_one)
        middle_low = middle.astype(BF16)
        hidden = dot(middle_low, up_weight) + up_shift
        share = 0.5 * lax.erfc(hidden * (-(0.5**0.5)))
        slope = share + hidden * jnp.exp(hidden * hidden * -0.5) * 0.3989422804014327
        active = (hidden * share).astype(BF16)
        second = middle + down_shift
        for at in range(chunks):
            second = second + dot(active[:, at * width : (at + 1) * width], down_weight[at])
        result, unit_two, inverse_two = norm_forward(second, gain_two, shift_two)
        layers.append(
            (
                layer_in,
                joint,
                out_weight,
                up_weight,
                down_weight,
                gain_one,
                gain_two,
                pairs,
                queries,
                mixed,
                lse,
                attended,
                unit_one,
                inverse_one,
                middle_low,
                slope,
                active,
                unit_two,
                inverse_two,
            )
        )
        layer_in = result.astype(BF16)
        outputs.append(layer_in)

    moves = [[(1, 0)], [(0, 1)]]

    def both_batches(value):
        got = across_half(value[rows:].astype(BF16)).astype(value.dtype)
        own = value[:rows]
        return jnp.stack([jnp.where(low_half, own, got), jnp.where(low_half, got, own)], axis=0)

    def placed(first, second):
        first_got = lax.ppermute(first.astype(BF16), "section", moves[0]).astype(first.dtype)
        second_got = lax.ppermute(second.astype(BF16), "section", moves[1]).astype(first.dtype)
        return jnp.where(
            first_section,
            jnp.concatenate([first, first_got], axis=0),
            jnp.concatenate([second_got, second], axis=0),
        )

    ready = [both_batches(value) for value in outputs]

    def reduced(value):
        return lax.psum_scatter(value, GROUP, scatter_dimension=0, tiled=True)

    wide_sums = [None, None]
    last_sums = [None, None]
    for layer in (1, 0):
        (
            layer_in,
            joint,
            out_weight,
            up_weight,
            down_weight,
            gain_one,
            gain_two,
            pairs,
            queries,
            mixed,
            lse,
            attended,
            unit_one,
            inverse_one,
            middle_low,
            slope,
            active,
            unit_two,
            inverse_two,
        ) = layers[layer]
        grad_second, grad_gain_two, grad_shift_two = norm_backward(
            grad_top, unit_two, inverse_two, gain_two
        )
        grad_down_low = grad_second.astype(BF16)
        grad_active = jnp.concatenate(
            [dot(grad_down_low, down_weight[at], NT) for at in range(chunks)], axis=1
        )
        grad_hidden = (grad_active * slope).astype(BF16)
        grad_down = [
            dot(active[:, at * width : (at + 1) * width], grad_down_low, TN).astype(BF16)
            for at in range(chunks)
        ]
        grad_up = dot(middle_low, grad_hidden, TN).astype(BF16)
        parts = [grad_up] + grad_down
        wide = jnp.concatenate(parts, axis=1)
        if layer == 0:
            grad_hidden, wide, wide_sums[1] = tied(grad_hidden, wide, wide_sums[1])
        else:
            grad_hidden, wide = tied(grad_hidden, wide)
        wide_sums[layer] = reduced(wide)
        grad_middle = grad_second + dot(grad_hidden, up_weight, NT)
        grad_first, grad_gain_one, grad_shift_one = norm_backward(
            grad_middle, unit_one, inverse_one, gain_one
        )
        grad_branch = grad_first.astype(BF16)
        grad_returned = dot(grad_branch, out_weight, NT).astype(BF16)
        grad_mixed = to_heads(columns(grad_returned, part_width))
        if direct and layer == 0:
            grad_mixed, *last_chip = tied(grad_mixed, *last_chip)
            last_side = side_sum(last_chip)[0]
        grad_queries, grad_pairs = attention_backward(
            queries, pairs, query_ids, key_marks, mixed, lse, grad_mixed
        )
        if direct and layer == 0:
            grad_queries, grad_pairs, last_side = tied(grad_queries, grad_pairs, last_side)
        grad_arrived = jnp.concatenate([own_keys_sum(grad_pairs), grad_queries], axis=1)
        grad_joint = jnp.concatenate(to_tokens(grad_arrived), axis=1)
        grad_input = grad_first + dot(grad_joint, joint, NT)
        joint_sum = jnp.sum(grad_joint.astype(F32), axis=0).reshape(members, 3, part_width)
        small = jnp.stack(
            [
                joint_sum[:, 2].reshape(width),
                joint_sum[:, 1].reshape(width),
                jnp.sum(grad_branch.astype(F32), axis=0),
                grad_gain_one,
                grad_shift_one,
                jnp.sum(grad_down_low.astype(F32), axis=0),
                grad_gain_two,
                grad_shift_two,
            ],
            axis=0,
        )
        hidden_sum = jnp.sum(grad_hidden.astype(F32), axis=0).reshape(chunks, width)
        small = jnp.concatenate([small, hidden_sum], axis=0).astype(BF16)
        small = jnp.pad(small.T, ((0, 0), (0, 128 - small_count)))
        if direct:
            last_chip = chip_parts(
                [
                    jnp.concatenate(group, axis=1)
                    for group in zip(
                        weight_grad(layer_in, grad_joint),
                        weight_grad(attended, grad_branch),
                        halves(small, 0),
                    )
                ]
            )
        else:
            last_sums[layer] = reduced(
                jnp.concatenate(
                    [
                        dot(layer_in, grad_joint, TN).astype(BF16),
                        dot(attended, grad_branch, TN).astype(BF16),
                        small,
                    ],
                    axis=1,
                )
            )
        ready.append(both_batches(grad_input))
        grad_top = grad_input.astype(BF16).astype(F32)

    def settle(first, second):
        to_first = lax.ppermute(first, "section", [(1, 0)])
        to_second = lax.ppermute(second, "section", [(0, 1)])
        return jnp.where(first_section, first, second).astype(F32) + jnp.where(
            first_section, to_first, to_second
        ).astype(F32)

    if direct:
        last_sides = jnp.concatenate([side_sum(last_chip)[0], last_side], axis=-1)
        last_sides, wide_sums[0], *ready = tied(last_sides, wide_sums[0], *ready)
        both = line_sum(last_sides)
        last_sums = [both[:, : both.shape[1] // 2], both[:, both.shape[1] // 2 :]]
    wide = settle(wide_sums[0], wide_sums[1])
    last = settle(last_sums[0], last_sums[1])
    grad_up = (
        wide[:, :hidden_width]
        .reshape(shard, chunks, head_count * blk_count, shard)
        .transpose(0, 2, 1, 3)
        .reshape(shard, hidden_width)
    )
    grad_down = jnp.concatenate(
        [
            wide[:, hidden_width + at * width : hidden_width + (at + 1) * width]
            for at in range(chunks)
        ],
        axis=0,
    )
    grad_joint = last[:, :joint_width].reshape(shard, members, 3, part_width)
    grad_key, grad_value, grad_query = [
        grad_joint[:, :, at].reshape(shard, width) for at in range(3)
    ]
    grad_out = last[:, 3 * width : 4 * width]
    small = last[:, 4 * width :].T

    outputs_all = placed(ready[0], ready[1])
    grad_inputs = placed(ready[3], ready[2])
    return (
        outputs_all[None],
        grad_inputs[None],
        grad_query[None],
        grad_key[None],
        grad_value[None],
        grad_out[None],
        small[0][None],
        small[1][None],
        small[2][None],
        small[3][None],
        small[4][None],
        grad_up[None],
        small[8 : 8 + chunks].reshape(1, chunks * shard),
        grad_down[None],
        small[5][None],
        small[6][None],
        small[7][None],
    )


def solution(mesh):
    rows = P(None, GROUP, None)
    marks = P(None, GROUP)
    matrix = P("section", GROUP, None)
    vector = P("section", GROUP)
    result = P("section", None, GROUP, None)
    return jax.shard_map(
        body,
        mesh=mesh,
        in_specs=(rows, rows, marks, marks)
        + (matrix,) * 4
        + (vector,) * 5
        + (matrix, vector, matrix, vector, vector, vector),
        out_specs=(result, result)
        + (matrix,) * 4
        + (vector,) * 5
        + (matrix, vector, matrix, vector, vector, vector),
        check_vma=False,
    )
```

```python
import functools

import jax
import jax.numpy as jnp
from jax import lax
from jax.experimental import pallas as pl
from jax.experimental.pallas import tpu as pltpu
from jax.sharding import PartitionSpec as P

HEAD_DIM = 64
GROUP = ("head", "blk")
F32 = jnp.float32
BF16 = jnp.bfloat16
NT = (((1,), (1,)), ((), ()))
NN = (((1,), (0,)), ((), ()))
TN = (((0,), (0,)), ((), ()))
VMEM_LIMIT = 48 * 1024 * 1024


def dot(left, right, dims=NN):
    return lax.dot_general(left, right, dims, preferred_element_type=F32)


def head_lanes(value, head):
    lane = lax.broadcasted_iota(jnp.int32, value.shape, 1)
    return jnp.where(lane // HEAD_DIM == head, value, jnp.zeros_like(value))


def attention_forward_kernel(q_ref, kv_ref, qid_ref, mark_ref, out_ref, lse_ref, qm, acc, top, total):
    step = pl.program_id(0)
    heads = qm.shape[0]
    width = q_ref.shape[1]

    @pl.when(step == 0)
    def _():
        scaled = q_ref[...] * jnp.asarray(0.125, BF16)
        for head in range(heads):
            qm[head] = head_lanes(scaled, head)
        acc[...] = jnp.zeros_like(acc)
        top[...] = jnp.full_like(top, -1e30)
        total[...] = jnp.zeros_like(total)

    keys = kv_ref[:, :width]
    values = kv_ref[:, width:]
    allowed = mark_ref[...] == qid_ref[...]
    for head in range(heads):
        scores = jnp.where(allowed, dot(keys, qm[head], NT), -1e30)
        before = top[head : head + 1]
        after = jnp.maximum(before, jnp.max(scores, axis=0, keepdims=True))
        weights = jnp.exp(scores - after)
        fade = jnp.exp(before - after)
        top[head : head + 1] = after
        total[head : head + 1] = total[head : head + 1] * fade + jnp.sum(weights, axis=0, keepdims=True)
        rows = slice(head * HEAD_DIM, (head + 1) * HEAD_DIM)
        part = dot(values, weights.astype(BF16), TN)
        acc[rows] = acc[rows] * fade + part[rows]

    @pl.when(step == pl.num_programs(0) - 1)
    def _():
        scale = 1.0 / total[:heads]
        parts = [
            acc[head * HEAD_DIM : (head + 1) * HEAD_DIM] * scale[head : head + 1] for head in range(heads)
        ]
        out_ref[...] = jnp.concatenate(parts, axis=0).T
        lse_ref[...] = top[...] + jnp.log(jnp.maximum(total[...], 1e-30))


def attention_backward_kernel(
    q_ref, kv_ref, qid_ref, mark_ref, out_ref, lse_ref, do_ref, dq_ref, dkv_ref, qm, dom, acc, delta
):
    step = pl.program_id(0)
    heads = qm.shape[0]
    width = q_ref.shape[1]

    @pl.when(step == 0)
    def _():
        scaled = q_ref[...] * jnp.asarray(0.125, BF16)
        incoming = do_ref[...]
        for head in range(heads):
            qm[head] = head_lanes(scaled, head)
            dom[head] = head_lanes(incoming, head)
        product = incoming.astype(F32) * out_ref[...]
        row = lax.broadcasted_iota(jnp.int32, (8, width), 0)
        lane = lax.broadcasted_iota(jnp.int32, (8, width), 1)
        chooser = jnp.where(lane // HEAD_DIM == row, 1.0, 0.0).astype(F32)
        delta[...] = lax.dot_general(
            chooser, product, NT, preferred_element_type=F32, precision=lax.Precision.HIGHEST
        )
        acc[...] = jnp.zeros_like(acc)

    keys = kv_ref[:, :width]
    values = kv_ref[:, width:]
    allowed = mark_ref[...] == qid_ref[...]
    grad_keys = jnp.zeros(keys.shape, F32)
    grad_values = jnp.zeros(keys.shape, F32)
    for head in range(heads):
        scores = dot(keys, qm[head], NT)
        weights = jnp.where(allowed, jnp.exp(scores - lse_ref[head : head + 1]), 0.0)
        grad_weights = dot(values, dom[head], NT)
        grad_scores = (weights * (grad_weights - delta[head : head + 1])).astype(BF16)
        grad_values += dot(weights.astype(BF16), dom[head])
        grad_keys += dot(grad_scores, qm[head])
        rows = slice(head * HEAD_DIM, (head + 1) * HEAD_DIM)
        acc[rows] += dot(keys, grad_scores, TN)[rows]
    dkv_ref[:, :width] = grad_keys.astype(BF16)
    dkv_ref[:, width:] = grad_values.astype(BF16)

    @pl.when(step == pl.num_programs(0) - 1)
    def _():
        dq_ref[...] = (acc[...] * 0.125).T.astype(BF16)


def key_block(count):
    return 256 if count % 256 == 0 else count


def whole(shape):
    return pl.BlockSpec(shape, lambda step: (0,) * len(shape))


def attention_cost(rows, count, width, products):
    return pl.CostEstimate(
        flops=products * 2 * rows * count * width,
        bytes_accessed=rows * width * 12 + count * width * 8,
        transcendentals=rows * count * (width // HEAD_DIM),
    )


def attention_forward(queries, pairs, query_ids, marks):
    rows, width = queries.shape
    count = pairs.shape[0]
    heads = width // HEAD_DIM
    block = key_block(count)
    return pl.pallas_call(
        attention_forward_kernel,
        grid=(count // block,),
        in_specs=[
            whole((rows, width)),
            pl.BlockSpec((block, 2 * width), lambda step: (step, 0)),
            whole((1, rows)),
            pl.BlockSpec((block, 1), lambda step: (step, 0)),
        ],
        out_specs=[whole((rows, width)), whole((8, rows))],
        out_shape=[
            jax.ShapeDtypeStruct((rows, width), F32),
            jax.ShapeDtypeStruct((8, rows), F32),
        ],
        scratch_shapes=[
            pltpu.VMEM((heads, rows, width), BF16),
            pltpu.VMEM((width, rows), F32),
            pltpu.VMEM((8, rows), F32),
            pltpu.VMEM((8, rows), F32),
        ],
        compiler_params=pltpu.CompilerParams(vmem_limit_bytes=VMEM_LIMIT),
        cost_estimate=attention_cost(rows, count, width, 28),
        name="attention_forward",
    )(queries, pairs, query_ids, marks)


def attention_backward(queries, pairs, query_ids, marks, out, lse, grad_out):
    rows, width = queries.shape
    count = pairs.shape[0]
    heads = width // HEAD_DIM
    block = key_block(count)
    return pl.pallas_call(
        attention_backward_kernel,
        grid=(count // block,),
        in_specs=[
            whole((rows, width)),
            pl.BlockSpec((block, 2 * width), lambda step: (step, 0)),
            whole((1, rows)),
            pl.BlockSpec((block, 1), lambda step: (step, 0)),
            whole((rows, width)),
            whole((8, rows)),
            whole((rows, width)),
        ],
        out_specs=[
            whole((rows, width)),
            pl.BlockSpec((block, 2 * width), lambda step: (step, 0)),
        ],
        out_shape=[
            jax.ShapeDtypeStruct((rows, width), BF16),
            jax.ShapeDtypeStruct((count, 2 * width), BF16),
        ],
        scratch_shapes=[
            pltpu.VMEM((heads, rows, width), BF16),
            pltpu.VMEM((heads, rows, width), BF16),
            pltpu.VMEM((width, rows), F32),
            pltpu.VMEM((8, rows), F32),
        ],
        compiler_params=pltpu.CompilerParams(vmem_limit_bytes=VMEM_LIMIT),
        cost_estimate=attention_cost(rows, count, width, 34),
        name="attention_backward",
    )(queries, pairs, query_ids, marks, out, lse, grad_out)


def norm_forward(value, gain, shift):
    centre = value - jnp.mean(value, axis=-1, keepdims=True)
    inverse = lax.rsqrt(jnp.mean(centre * centre, axis=-1, keepdims=True) + 1e-05)
    unit = centre * inverse
    return unit * gain + shift, unit, inverse


def norm_backward(grad, unit, inverse, gain):
    scaled = grad * gain
    mean_one = jnp.mean(scaled, axis=-1, keepdims=True)
    mean_two = jnp.mean(scaled * unit, axis=-1, keepdims=True)
    return (
        inverse * (scaled - mean_one - unit * mean_two),
        jnp.sum(grad * unit, axis=0),
        jnp.sum(grad, axis=0),
    )


def body(
    tokens,
    cotangent,
    doc_ids,
    pad_mask,
    w_query,
    w_key,
    w_value,
    w_out,
    b_query,
    b_value,
    b_out,
    gain_attn,
    bias_attn,
    w_up,
    b_up,
    w_down,
    b_down,
    gain_ffn,
    bias_ffn,
):
    section = lax.axis_index("section")
    head_count = lax.axis_size("head")
    blk_count = lax.axis_size("blk")
    head_at = lax.axis_index("head")
    blk_at = lax.axis_index("blk")
    batches, rows, width = tokens.shape
    shard = width // (head_count * blk_count)
    hidden_width = w_up.shape[2]
    chunks = hidden_width // width
    half = blk_count // 2
    middles = blk_count // 4
    per_section = batches // 2
    members = 4
    part_width = width // members
    pair_width = 2 * part_width
    first_section = section == 0
    low_half = blk_at < half
    member = (head_at // 2) * 2 + blk_at % 2
    own_batch = section * per_section + blk_at // half
    other_batch = section * per_section + 1 - blk_at // half

    def across_section(value):
        return lax.ppermute(value, "section", [(0, 1), (1, 0)])

    def across_half(value):
        return lax.ppermute(value, "blk", [(at, (at + half) % blk_count) for at in range(blk_count)])

    def across_member(value, step):
        pairs = []
        for head in range(head_count):
            for blk in range(blk_count):
                there = (head ^ (step & 2)) * blk_count + (blk ^ (step & 1))
                pairs.append((head * blk_count + blk, there))
        return lax.ppermute(value, GROUP, pairs)

    def across_core(value):
        return lax.ppermute(value, "head", [(at, at ^ 1) for at in range(head_count)])

    def across_middle(value, step):
        pairs = []
        for at in range(blk_count):
            base, middle, low = at // half, (at % half) // 2, at % 2
            pairs.append((at, base * half + ((middle + step) % middles) * 2 + low))
        return lax.ppermute(value, "blk", pairs)

    direct = head_count == 4 and blk_count == 4
    core_at = head_at % 2
    side_at = head_at // 2

    def across_side(value):
        return lax.ppermute(value, "head", [(at, at ^ 2) for at in range(head_count)])

    def add(*values):
        return sum(value.astype(F32) for value in values).astype(BF16)

    def tied(*values):
        return lax.optimization_barrier(values)

    def halves(value, axis):
        shape = value.shape
        lead = shape[axis] // width
        split = value.reshape(shape[:axis] + (lead, 2, 2, width // 4) + shape[axis + 1 :])
        first = lax.index_in_dim(split, 0, axis + 2, keepdims=False)
        second = lax.index_in_dim(split, 1, axis + 2, keepdims=False)
        flat = shape[:axis] + (shape[axis] // 2,) + shape[axis + 1 :]
        return (
            jnp.where(core_at == 0, first, second).reshape(flat),
            jnp.where(core_at == 0, second, first).reshape(flat),
        )

    def weight_grad(left, right):
        return [dot(part, right, TN).astype(BF16) for part in halves(left, 1)]

    def chip_parts(parts):
        return [parts[0], across_core(parts[1])]

    def side_sum(parts):
        views = [part.reshape(-1, 2, blk_count, shard, part.shape[1]) for part in parts]

        def at(which):
            return [lax.dynamic_index_in_dim(view, which, 1, keepdims=False) for view in views]

        return add(*at(side_at), across_side(add(*at(1 - side_at))))

    def line_sum(value):
        return lax.psum_scatter(value, "blk", scatter_dimension=0, tiled=True)[0]

    def pick(value, at):
        return lax.dynamic_index_in_dim(value, at, 0, keepdims=False)

    def to_heads(groups):
        own = [pick(groups, member ^ step) for step in range(members)]
        return jnp.concatenate(
            [own[0]] + [across_member(own[step], step) for step in range(1, members)], axis=0
        )

    def to_tokens(value):
        parts = value.reshape(members, value.shape[0] // members, value.shape[1])
        back = jnp.stack(
            [parts[0]] + [across_member(parts[step], step) for step in range(1, members)], axis=0
        )
        return [pick(back, member ^ at) for at in range(members)]

    def all_keys(value):
        value = jnp.concatenate([value, across_core(value)], axis=0)
        return jnp.concatenate(
            [value] + [across_middle(value, step) for step in range(1, middles)], axis=0
        )

    def own_keys_sum(value):
        count = value.shape[0] // middles
        total = value[:count].astype(F32)
        for step in range(1, middles):
            back = across_middle(value[step * count : (step + 1) * count], middles - step)
            total = total + back.astype(F32)
        partner = across_core(total[count // 2 :].astype(BF16))
        return (total[: count // 2] + partner.astype(F32)).astype(BF16)

    def columns(value, size):
        return value.reshape(value.shape[0], members, size).transpose(1, 0, 2)

    def split_parts(value):
        return value[0].reshape(shard, members, part_width)

    joint_local = jnp.concatenate(
        [split_parts(w_key), split_parts(w_value), split_parts(w_query)], axis=2
    )
    small_local = jnp.stack(
        [
            part.reshape(shard)
            for part in (b_query, b_value, b_out, gain_attn, bias_attn, b_down, gain_ffn, bias_ffn)
        ]
        + [b_up[0].reshape(chunks, shard)[at] for at in range(chunks)],
        axis=1,
    )
    small_count = small_local.shape[1]
    joint_width = 3 * width
    first_local = jnp.concatenate(
        [
            joint_local.reshape(shard, joint_width),
            jnp.pad(small_local, ((0, 0), (0, 128 - small_count))),
        ],
        axis=1,
    )
    up_local = (
        w_up[0]
        .reshape(shard, head_count * blk_count, chunks, shard)
        .transpose(0, 2, 1, 3)
        .reshape(shard, hidden_width)
    )
    down_local = jnp.concatenate(
        [w_down[0, at * shard : (at + 1) * shard] for at in range(chunks)], axis=1
    )
    rest_local = jnp.concatenate([w_out[0], up_local, down_local], axis=1)
    rest_other = across_section(rest_local)
    first_all = lax.all_gather(first_local, ("section",) + GROUP, axis=0, tiled=True)
    rest_all = [
        lax.all_gather(
            jnp.where(first_section, rest_local, rest_other), GROUP, axis=0, tiled=True
        ),
        lax.all_gather(
            jnp.where(first_section, rest_other, rest_local), GROUP, axis=0, tiled=True
        ),
    ]

    def both_blocks(value):
        return jnp.concatenate(
            [pick(value, own_batch), across_half(pick(value, other_batch))], axis=0
        )

    layer_in = both_blocks(tokens)
    grad_top = both_blocks(cotangent)
    marks_local = jnp.where(pad_mask == 1, doc_ids, -1)
    labels = both_blocks(jnp.stack([doc_ids, marks_local], axis=-1))
    labels = jnp.concatenate(
        [labels] + [across_member(labels, step) for step in range(1, members)], axis=0
    )
    query_ids = labels[:, 0].reshape(1, -1)
    key_marks = all_keys(labels)[:, 1].reshape(-1, 1)

    layers = []
    outputs = []
    for layer in range(2):
        joint = first_all[layer * width : (layer + 1) * width, :joint_width]
        small = first_all[layer * width : (layer + 1) * width, joint_width:].T.astype(F32)
        rest = rest_all[layer]
        out_weight = rest[:, :width]
        up_weight = rest[:, width : width + hidden_width]
        down_weight = [
            rest[:, width + hidden_width + at * width : width + hidden_width + (at + 1) * width]
            for at in range(chunks)
        ]
        q_shift, v_shift, out_shift, gain_one, shift_one, down_shift, gain_two, shift_two = [
            small[at] for at in range(8)
        ]
        up_shift = small[8 : 8 + chunks].reshape(hidden_width)
        joint_shift = jnp.concatenate(
            [
                jnp.zeros((members, part_width), F32),
                v_shift.reshape(members, part_width),
                q_shift.reshape(members, part_width),
            ],
            axis=1,
        )
        joint_rows = (dot(layer_in, joint) + joint_shift.reshape(joint_width)).astype(BF16)
        arrived = to_heads(columns(joint_rows, pair_width + part_width))
        pairs = all_keys(arrived[:, :pair_width])
        queries = arrived[:, pair_width:]
        mixed, lse = attention_forward(queries, pairs, query_ids, key_marks)
        attended = jnp.concatenate(to_tokens(mixed.astype(BF16)), axis=1)
        first_sum = layer_in.astype(F32) + dot(attended, out_weight) + out_shift
        middle, unit_one, inverse_one = norm_forward(first_sum, gain_one, shift_one)
        middle_low = middle.astype(BF16)
        hidden = dot(middle_low, up_weight) + up_shift
        share = 0.5 + 0.5 * lax.erf(hidden * 0.5**0.5)
        slope = share + hidden * jnp.exp(hidden * hidden * -0.5) * 0.3989422804014327
        active = (hidden * share).astype(BF16)
        second = middle + down_shift
        for at in range(chunks):
            second = second + dot(active[:, at * width : (at + 1) * width], down_weight[at])
        result, unit_two, inverse_two = norm_forward(second, gain_two, shift_two)
        layers.append(
            (
                layer_in,
                joint,
                out_weight,
                up_weight,
                down_weight,
                gain_one,
                gain_two,
                pairs,
                queries,
                mixed,
                lse,
                attended,
                unit_one,
                inverse_one,
                middle_low,
                slope,
                active,
                unit_two,
                inverse_two,
            )
        )
        layer_in = result.astype(BF16)
        outputs.append(layer_in)

    moves = [[(1, 0)], [(0, 1)]]

    def both_batches(value):
        got = across_half(value[rows:].astype(BF16)).astype(value.dtype)
        own = value[:rows]
        return jnp.stack([jnp.where(low_half, own, got), jnp.where(low_half, got, own)], axis=0)

    def placed(first, second):
        first_got = lax.ppermute(first.astype(BF16), "section", moves[0]).astype(first.dtype)
        second_got = lax.ppermute(second.astype(BF16), "section", moves[1]).astype(first.dtype)
        return jnp.where(
            first_section,
            jnp.concatenate([first, first_got], axis=0),
            jnp.concatenate([second_got, second], axis=0),
        )

    ready = [both_batches(value) for value in outputs]

    def reduced(value):
        return lax.psum_scatter(value, GROUP, scatter_dimension=0, tiled=True)

    wide_sums = [None, None]
    last_sums = [None, None]
    for layer in (1, 0):
        (
            layer_in,
            joint,
            out_weight,
            up_weight,
            down_weight,
            gain_one,
            gain_two,
            pairs,
            queries,
            mixed,
            lse,
            attended,
            unit_one,
            inverse_one,
            middle_low,
            slope,
            active,
            unit_two,
            inverse_two,
        ) = layers[layer]
        grad_second, grad_gain_two, grad_shift_two = norm_backward(
            grad_top, unit_two, inverse_two, gain_two
        )
        grad_down_low = grad_second.astype(BF16)
        grad_active = jnp.concatenate(
            [dot(grad_down_low, down_weight[at], NT) for at in range(chunks)], axis=1
        )
        grad_hidden = (grad_active * slope).astype(BF16)
        grad_down = [
            dot(active[:, at * width : (at + 1) * width], grad_down_low, TN).astype(BF16)
            for at in range(chunks)
        ]
        grad_up = dot(middle_low, grad_hidden, TN).astype(BF16)
        parts = [grad_up] + grad_down
        wide = jnp.concatenate(parts, axis=1)
        if layer == 0:
            grad_hidden, wide, wide_sums[1] = tied(grad_hidden, wide, wide_sums[1])
        else:
            grad_hidden, wide = tied(grad_hidden, wide)
        wide_sums[layer] = reduced(wide)
        grad_middle = grad_second + dot(grad_hidden, up_weight, NT)
        grad_first, grad_gain_one, grad_shift_one = norm_backward(
            grad_middle, unit_one, inverse_one, gain_one
        )
        grad_branch = grad_first.astype(BF16)
        grad_returned = dot(grad_branch, out_weight, NT).astype(BF16)
        grad_mixed = to_heads(columns(grad_returned, part_width))
        if direct and layer == 0:
            grad_mixed, *last_chip = tied(grad_mixed, *last_chip)
            last_side = side_sum(last_chip)[0]
        grad_queries, grad_pairs = attention_backward(
            queries, pairs, query_ids, key_marks, mixed, lse, grad_mixed
        )
        if direct and layer == 0:
            grad_queries, grad_pairs, last_side = tied(grad_queries, grad_pairs, last_side)
        grad_arrived = jnp.concatenate([own_keys_sum(grad_pairs), grad_queries], axis=1)
        grad_joint = jnp.concatenate(to_tokens(grad_arrived), axis=1)
        grad_input = grad_first + dot(grad_joint, joint, NT)
        joint_sum = jnp.sum(grad_joint.astype(F32), axis=0).reshape(members, 3, part_width)
        small = jnp.stack(
            [
                joint_sum[:, 2].reshape(width),
                joint_sum[:, 1].reshape(width),
                jnp.sum(grad_branch.astype(F32), axis=0),
                grad_gain_one,
                grad_shift_one,
                jnp.sum(grad_down_low.astype(F32), axis=0),
                grad_gain_two,
                grad_shift_two,
            ],
            axis=0,
        )
        hidden_sum = jnp.sum(grad_hidden.astype(F32), axis=0).reshape(chunks, width)
        small = jnp.concatenate([small, hidden_sum], axis=0).astype(BF16)
        small = jnp.pad(small.T, ((0, 0), (0, 128 - small_count)))
        if direct:
            last_chip = chip_parts(
                [
                    jnp.concatenate(group, axis=1)
                    for group in zip(
                        weight_grad(layer_in, grad_joint),
                        weight_grad(attended, grad_branch),
                        halves(small, 0),
                    )
                ]
            )
        else:
            last_sums[layer] = reduced(
                jnp.concatenate(
                    [
                        dot(layer_in, grad_joint, TN).astype(BF16),
                        dot(attended, grad_branch, TN).astype(BF16),
                        small,
                    ],
                    axis=1,
                )
            )
        ready.append(both_batches(grad_input))
        grad_top = grad_input.astype(BF16).astype(F32)

    def settle(first, second):
        to_first = lax.ppermute(first, "section", [(1, 0)])
        to_second = lax.ppermute(second, "section", [(0, 1)])
        return jnp.where(first_section, first, second).astype(F32) + jnp.where(
            first_section, to_first, to_second
        ).astype(F32)

    if direct:
        last_sides = jnp.concatenate([side_sum(last_chip)[0], last_side], axis=-1)
        last_sides, wide_sums[0], *ready[:3] = tied(last_sides, wide_sums[0], *ready[:3])
        both = line_sum(last_sides)
        last_sums = [both[:, : both.shape[1] // 2], both[:, both.shape[1] // 2 :]]
    wide = settle(wide_sums[0], wide_sums[1])
    last = settle(last_sums[0], last_sums[1])
    grad_up = (
        wide[:, :hidden_width]
        .reshape(shard, chunks, head_count * blk_count, shard)
        .transpose(0, 2, 1, 3)
        .reshape(shard, hidden_width)
    )
    grad_down = jnp.concatenate(
        [
            wide[:, hidden_width + at * width : hidden_width + (at + 1) * width]
            for at in range(chunks)
        ],
        axis=0,
    )
    grad_joint = last[:, :joint_width].reshape(shard, members, 3, part_width)
    grad_key, grad_value, grad_query = [
        grad_joint[:, :, at].reshape(shard, width) for at in range(3)
    ]
    grad_out = last[:, 3 * width : 4 * width]
    small = last[:, 4 * width :].T

    outputs_all = placed(ready[0], ready[1])
    grad_inputs = placed(ready[3], ready[2])
    return (
        outputs_all[None],
        grad_inputs[None],
        grad_query[None],
        grad_key[None],
        grad_value[None],
        grad_out[None],
        small[0][None],
        small[1][None],
        small[2][None],
        small[3][None],
        small[4][None],
        grad_up[None],
        small[8 : 8 + chunks].reshape(1, chunks * shard),
        grad_down[None],
        small[5][None],
        small[6][None],
        small[7][None],
    )


def solution(mesh):
    rows = P(None, GROUP, None)
    marks = P(None, GROUP)
    matrix = P("section", GROUP, None)
    vector = P("section", GROUP)
    result = P("section", None, GROUP, None)
    return jax.shard_map(
        body,
        mesh=mesh,
        in_specs=(rows, rows, marks, marks)
        + (matrix,) * 4
        + (vector,) * 5
        + (matrix, vector, matrix, vector, vector, vector),
        out_specs=(result, result)
        + (matrix,) * 4
        + (vector,) * 5
        + (matrix, vector, matrix, vector, vector, vector),
        check_vma=False,
    )
```

```python
import functools

import jax
import jax.numpy as jnp
from jax import lax
from jax.experimental import pallas as pl
from jax.experimental.pallas import tpu as pltpu
from jax.sharding import PartitionSpec as P

HEAD_DIM = 64
GROUP = ("head", "blk")
F32 = jnp.float32
BF16 = jnp.bfloat16
NT = (((1,), (1,)), ((), ()))
NN = (((1,), (0,)), ((), ()))
TN = (((0,), (0,)), ((), ()))
VMEM_LIMIT = 48 * 1024 * 1024


def dot(left, right, dims=NN):
    return lax.dot_general(left, right, dims, preferred_element_type=F32)


def head_lanes(value, head):
    lane = lax.broadcasted_iota(jnp.int32, value.shape, 1)
    return jnp.where(lane // HEAD_DIM == head, value, jnp.zeros_like(value))


def attention_forward_kernel(q_ref, kv_ref, qid_ref, mark_ref, out_ref, lse_ref, qm, acc, top, total):
    step = pl.program_id(0)
    heads = qm.shape[0]
    width = q_ref.shape[1]

    @pl.when(step == 0)
    def _():
        scaled = q_ref[...] * jnp.asarray(0.125, BF16)
        for head in range(heads):
            qm[head] = head_lanes(scaled, head)
        acc[...] = jnp.zeros_like(acc)
        top[...] = jnp.full_like(top, -1e30)
        total[...] = jnp.zeros_like(total)

    keys = kv_ref[:, :width]
    values = kv_ref[:, width:]
    allowed = mark_ref[...] == qid_ref[...]
    for head in range(heads):
        scores = jnp.where(allowed, dot(keys, qm[head], NT), -1e30)
        before = top[head : head + 1]
        after = jnp.maximum(before, jnp.max(scores, axis=0, keepdims=True))
        weights = jnp.exp(scores - after)
        fade = jnp.exp(before - after)
        top[head : head + 1] = after
        total[head : head + 1] = total[head : head + 1] * fade + jnp.sum(weights, axis=0, keepdims=True)
        rows = slice(head * HEAD_DIM, (head + 1) * HEAD_DIM)
        part = dot(values, weights.astype(BF16), TN)
        acc[rows] = acc[rows] * fade + part[rows]

    @pl.when(step == pl.num_programs(0) - 1)
    def _():
        scale = 1.0 / total[:heads]
        parts = [
            acc[head * HEAD_DIM : (head + 1) * HEAD_DIM] * scale[head : head + 1] for head in range(heads)
        ]
        out_ref[...] = jnp.concatenate(parts, axis=0).T
        lse_ref[...] = top[...] + jnp.log(jnp.maximum(total[...], 1e-30))


def attention_backward_kernel(
    q_ref, kv_ref, qid_ref, mark_ref, out_ref, lse_ref, do_ref, dq_ref, dkv_ref, qm, dom, acc, delta
):
    step = pl.program_id(0)
    heads = qm.shape[0]
    width = q_ref.shape[1]

    @pl.when(step == 0)
    def _():
        scaled = q_ref[...] * jnp.asarray(0.125, BF16)
        incoming = do_ref[...]
        for head in range(heads):
            qm[head] = head_lanes(scaled, head)
            dom[head] = head_lanes(incoming, head)
        product = incoming.astype(F32) * out_ref[...]
        row = lax.broadcasted_iota(jnp.int32, (8, width), 0)
        lane = lax.broadcasted_iota(jnp.int32, (8, width), 1)
        chooser = jnp.where(lane // HEAD_DIM == row, 1.0, 0.0).astype(F32)
        delta[...] = lax.dot_general(
            chooser, product, NT, preferred_element_type=F32, precision=lax.Precision.HIGHEST
        )
        acc[...] = jnp.zeros_like(acc)

    keys = kv_ref[:, :width]
    values = kv_ref[:, width:]
    allowed = mark_ref[...] == qid_ref[...]
    grad_keys = jnp.zeros(keys.shape, F32)
    grad_values = jnp.zeros(keys.shape, F32)
    for head in range(heads):
        scores = dot(keys, qm[head], NT)
        weights = jnp.where(allowed, jnp.exp(scores - lse_ref[head : head + 1]), 0.0)
        grad_weights = dot(values, dom[head], NT)
        grad_scores = (weights * (grad_weights - delta[head : head + 1])).astype(BF16)
        grad_values += dot(weights.astype(BF16), dom[head])
        grad_keys += dot(grad_scores, qm[head])
        rows = slice(head * HEAD_DIM, (head + 1) * HEAD_DIM)
        acc[rows] += dot(keys, grad_scores, TN)[rows]
    dkv_ref[:, :width] = grad_keys.astype(BF16)
    dkv_ref[:, width:] = grad_values.astype(BF16)

    @pl.when(step == pl.num_programs(0) - 1)
    def _():
        dq_ref[...] = (acc[...] * 0.125).T.astype(BF16)


def key_block(count):
    return 256 if count % 256 == 0 else count


def whole(shape):
    return pl.BlockSpec(shape, lambda step: (0,) * len(shape))


def attention_cost(rows, count, width, products):
    return pl.CostEstimate(
        flops=products * 2 * rows * count * width,
        bytes_accessed=rows * width * 12 + count * width * 8,
        transcendentals=rows * count * (width // HEAD_DIM),
    )


def attention_forward(queries, pairs, query_ids, marks):
    rows, width = queries.shape
    count = pairs.shape[0]
    heads = width // HEAD_DIM
    block = key_block(count)
    return pl.pallas_call(
        attention_forward_kernel,
        grid=(count // block,),
        in_specs=[
            whole((rows, width)),
            pl.BlockSpec((block, 2 * width), lambda step: (step, 0)),
            whole((1, rows)),
            pl.BlockSpec((block, 1), lambda step: (step, 0)),
        ],
        out_specs=[whole((rows, width)), whole((8, rows))],
        out_shape=[
            jax.ShapeDtypeStruct((rows, width), F32),
            jax.ShapeDtypeStruct((8, rows), F32),
        ],
        scratch_shapes=[
            pltpu.VMEM((heads, rows, width), BF16),
            pltpu.VMEM((width, rows), F32),
            pltpu.VMEM((8, rows), F32),
            pltpu.VMEM((8, rows), F32),
        ],
        compiler_params=pltpu.CompilerParams(vmem_limit_bytes=VMEM_LIMIT),
        cost_estimate=attention_cost(rows, count, width, 28),
        name="attention_forward",
    )(queries, pairs, query_ids, marks)


def attention_backward(queries, pairs, query_ids, marks, out, lse, grad_out):
    rows, width = queries.shape
    count = pairs.shape[0]
    heads = width // HEAD_DIM
    block = key_block(count)
    return pl.pallas_call(
        attention_backward_kernel,
        grid=(count // block,),
        in_specs=[
            whole((rows, width)),
            pl.BlockSpec((block, 2 * width), lambda step: (step, 0)),
            whole((1, rows)),
            pl.BlockSpec((block, 1), lambda step: (step, 0)),
            whole((rows, width)),
            whole((8, rows)),
            whole((rows, width)),
        ],
        out_specs=[
            whole((rows, width)),
            pl.BlockSpec((block, 2 * width), lambda step: (step, 0)),
        ],
        out_shape=[
            jax.ShapeDtypeStruct((rows, width), BF16),
            jax.ShapeDtypeStruct((count, 2 * width), BF16),
        ],
        scratch_shapes=[
            pltpu.VMEM((heads, rows, width), BF16),
            pltpu.VMEM((heads, rows, width), BF16),
            pltpu.VMEM((width, rows), F32),
            pltpu.VMEM((8, rows), F32),
        ],
        compiler_params=pltpu.CompilerParams(vmem_limit_bytes=VMEM_LIMIT),
        cost_estimate=attention_cost(rows, count, width, 34),
        name="attention_backward",
    )(queries, pairs, query_ids, marks, out, lse, grad_out)


def norm_forward(value, gain, shift):
    centre = value - jnp.mean(value, axis=-1, keepdims=True)
    inverse = lax.rsqrt(jnp.mean(centre * centre, axis=-1, keepdims=True) + 1e-05)
    unit = centre * inverse
    return unit * gain + shift, unit, inverse


def norm_backward(grad, unit, inverse, gain):
    scaled = grad * gain
    mean_one = jnp.mean(scaled, axis=-1, keepdims=True)
    mean_two = jnp.mean(scaled * unit, axis=-1, keepdims=True)
    return (
        inverse * (scaled - mean_one - unit * mean_two),
        jnp.sum(grad * unit, axis=0),
        jnp.sum(grad, axis=0),
    )


def body(
    tokens,
    cotangent,
    doc_ids,
    pad_mask,
    w_query,
    w_key,
    w_value,
    w_out,
    b_query,
    b_value,
    b_out,
    gain_attn,
    bias_attn,
    w_up,
    b_up,
    w_down,
    b_down,
    gain_ffn,
    bias_ffn,
):
    section = lax.axis_index("section")
    head_count = lax.axis_size("head")
    blk_count = lax.axis_size("blk")
    head_at = lax.axis_index("head")
    blk_at = lax.axis_index("blk")
    batches, rows, width = tokens.shape
    shard = width // (head_count * blk_count)
    hidden_width = w_up.shape[2]
    chunks = hidden_width // width
    half = blk_count // 2
    middles = blk_count // 4
    per_section = batches // 2
    members = 4
    part_width = width // members
    pair_width = 2 * part_width
    first_section = section == 0
    low_half = blk_at < half
    member = (head_at // 2) * 2 + blk_at % 2
    own_batch = section * per_section + blk_at // half
    other_batch = section * per_section + 1 - blk_at // half

    def across_section(value):
        return lax.ppermute(value, "section", [(0, 1), (1, 0)])

    def across_half(value):
        return lax.ppermute(value, "blk", [(at, (at + half) % blk_count) for at in range(blk_count)])

    def across_member(value, step):
        pairs = []
        for head in range(head_count):
            for blk in range(blk_count):
                there = (head ^ (step & 2)) * blk_count + (blk ^ (step & 1))
                pairs.append((head * blk_count + blk, there))
        return lax.ppermute(value, GROUP, pairs)

    def across_core(value):
        return lax.ppermute(value, "head", [(at, at ^ 1) for at in range(head_count)])

    def across_middle(value, step):
        pairs = []
        for at in range(blk_count):
            base, middle, low = at // half, (at % half) // 2, at % 2
            pairs.append((at, base * half + ((middle + step) % middles) * 2 + low))
        return lax.ppermute(value, "blk", pairs)

    direct = head_count == 4 and blk_count == 4
    core_at = head_at % 2
    side_at = head_at // 2

    def across_side(value):
        return lax.ppermute(value, "head", [(at, at ^ 2) for at in range(head_count)])

    def add(*values):
        return sum(value.astype(F32) for value in values).astype(BF16)

    def tied(*values):
        return lax.optimization_barrier(values)

    def halves(value, axis):
        shape = value.shape
        lead = shape[axis] // width
        split = value.reshape(shape[:axis] + (lead, 2, 2, width // 4) + shape[axis + 1 :])
        first = lax.index_in_dim(split, 0, axis + 2, keepdims=False)
        second = lax.index_in_dim(split, 1, axis + 2, keepdims=False)
        flat = shape[:axis] + (shape[axis] // 2,) + shape[axis + 1 :]
        return (
            jnp.where(core_at == 0, first, second).reshape(flat),
            jnp.where(core_at == 0, second, first).reshape(flat),
        )

    def weight_grad(left, right):
        return [dot(part, right, TN).astype(BF16) for part in halves(left, 1)]

    def chip_parts(parts):
        return [parts[0], across_core(parts[1])]

    def side_sum(parts):
        views = [part.reshape(-1, 2, blk_count, shard, part.shape[1]) for part in parts]

        def at(which):
            return [lax.dynamic_index_in_dim(view, which, 1, keepdims=False) for view in views]

        return add(*at(side_at), across_side(add(*at(1 - side_at))))

    def line_sum(value):
        return lax.psum_scatter(value, "blk", scatter_dimension=0, tiled=True)[0]

    def pick(value, at):
        return lax.dynamic_index_in_dim(value, at, 0, keepdims=False)

    def to_heads(groups):
        own = [pick(groups, member ^ step) for step in range(members)]
        return jnp.concatenate(
            [own[0]] + [across_member(own[step], step) for step in range(1, members)], axis=0
        )

    def to_tokens(value):
        parts = value.reshape(members, value.shape[0] // members, value.shape[1])
        back = jnp.stack(
            [parts[0]] + [across_member(parts[step], step) for step in range(1, members)], axis=0
        )
        return [pick(back, member ^ at) for at in range(members)]

    def all_keys(value):
        value = jnp.concatenate([value, across_core(value)], axis=0)
        return jnp.concatenate(
            [value] + [across_middle(value, step) for step in range(1, middles)], axis=0
        )

    def own_keys_sum(value):
        count = value.shape[0] // middles
        total = value[:count].astype(F32)
        for step in range(1, middles):
            back = across_middle(value[step * count : (step + 1) * count], middles - step)
            total = total + back.astype(F32)
        partner = across_core(total[count // 2 :].astype(BF16))
        return (total[: count // 2] + partner.astype(F32)).astype(BF16)

    def columns(value, size):
        return value.reshape(value.shape[0], members, size).transpose(1, 0, 2)

    def split_parts(value):
        return value[0].reshape(shard, members, part_width)

    joint_local = jnp.concatenate(
        [split_parts(w_key), split_parts(w_value), split_parts(w_query)], axis=2
    )
    small_local = jnp.stack(
        [
            part.reshape(shard)
            for part in (b_query, b_value, b_out, gain_attn, bias_attn, b_down, gain_ffn, bias_ffn)
        ]
        + [b_up[0].reshape(chunks, shard)[at] for at in range(chunks)],
        axis=1,
    )
    small_count = small_local.shape[1]
    joint_width = 3 * width
    first_local = jnp.concatenate(
        [
            joint_local.reshape(shard, joint_width),
            jnp.pad(small_local, ((0, 0), (0, 128 - small_count))),
        ],
        axis=1,
    )
    up_local = (
        w_up[0]
        .reshape(shard, head_count * blk_count, chunks, shard)
        .transpose(0, 2, 1, 3)
        .reshape(shard, hidden_width)
    )
    down_local = jnp.concatenate(
        [w_down[0, at * shard : (at + 1) * shard] for at in range(chunks)], axis=1
    )
    rest_local = jnp.concatenate([w_out[0], up_local, down_local], axis=1)
    rest_other = across_section(rest_local)
    first_all = lax.all_gather(first_local, ("section",) + GROUP, axis=0, tiled=True)
    rest_all = [
        lax.all_gather(
            jnp.where(first_section, rest_local, rest_other), GROUP, axis=0, tiled=True
        ),
        lax.all_gather(
            jnp.where(first_section, rest_other, rest_local), GROUP, axis=0, tiled=True
        ),
    ]

    def both_blocks(value):
        return jnp.concatenate(
            [pick(value, own_batch), across_half(pick(value, other_batch))], axis=0
        )

    layer_in = both_blocks(tokens)
    grad_top = both_blocks(cotangent)
    marks_local = jnp.where(pad_mask == 1, doc_ids, -1)
    labels = both_blocks(jnp.stack([doc_ids, marks_local], axis=-1))
    labels = jnp.concatenate(
        [labels] + [across_member(labels, step) for step in range(1, members)], axis=0
    )
    query_ids = labels[:, 0].reshape(1, -1)
    key_marks = all_keys(labels)[:, 1].reshape(-1, 1)

    layers = []
    outputs = []
    for layer in range(2):
        joint = first_all[layer * width : (layer + 1) * width, :joint_width]
        small = first_all[layer * width : (layer + 1) * width, joint_width:].T.astype(F32)
        rest = rest_all[layer]
        out_weight = rest[:, :width]
        up_weight = rest[:, width : width + hidden_width]
        down_weight = [
            rest[:, width + hidden_width + at * width : width + hidden_width + (at + 1) * width]
            for at in range(chunks)
        ]
        q_shift, v_shift, out_shift, gain_one, shift_one, down_shift, gain_two, shift_two = [
            small[at] for at in range(8)
        ]
        up_shift = small[8 : 8 + chunks].reshape(hidden_width)
        joint_shift = jnp.concatenate(
            [
                jnp.zeros((members, part_width), F32),
                v_shift.reshape(members, part_width),
                q_shift.reshape(members, part_width),
            ],
            axis=1,
        )
        joint_rows = (dot(layer_in, joint) + joint_shift.reshape(joint_width)).astype(BF16)
        arrived = to_heads(columns(joint_rows, pair_width + part_width))
        pairs = all_keys(arrived[:, :pair_width])
        queries = arrived[:, pair_width:]
        mixed, lse = attention_forward(queries, pairs, query_ids, key_marks)
        attended = jnp.concatenate(to_tokens(mixed.astype(BF16)), axis=1)
        first_sum = layer_in.astype(F32) + dot(attended, out_weight) + out_shift
        middle, unit_one, inverse_one = norm_forward(first_sum, gain_one, shift_one)
        middle_low = middle.astype(BF16)
        hidden = dot(middle_low, up_weight) + up_shift
        share = 0.5 + 0.5 * lax.erf(hidden * 0.5**0.5)
        slope = share + hidden * jnp.exp(hidden * hidden * -0.5) * 0.3989422804014327
        active = (hidden * share).astype(BF16)
        second = middle + down_shift
        for at in range(chunks):
            second = second + dot(active[:, at * width : (at + 1) * width], down_weight[at])
        result, unit_two, inverse_two = norm_forward(second, gain_two, shift_two)
        layers.append(
            (
                layer_in,
                joint,
                out_weight,
                up_weight,
                down_weight,
                gain_one,
                gain_two,
                pairs,
                queries,
                mixed,
                lse,
                attended,
                unit_one,
                inverse_one,
                middle_low,
                slope,
                active,
                unit_two,
                inverse_two,
            )
        )
        layer_in = result.astype(BF16)
        outputs.append(layer_in)

    moves = [[(1, 0)], [(0, 1)]]

    def both_batches(value):
        got = across_half(value[rows:].astype(BF16)).astype(value.dtype)
        own = value[:rows]
        return jnp.stack([jnp.where(low_half, own, got), jnp.where(low_half, got, own)], axis=0)

    def placed(first, second):
        first_got = lax.ppermute(first.astype(BF16), "section", moves[0]).astype(first.dtype)
        second_got = lax.ppermute(second.astype(BF16), "section", moves[1]).astype(first.dtype)
        return jnp.where(
            first_section,
            jnp.concatenate([first, first_got], axis=0),
            jnp.concatenate([second_got, second], axis=0),
        )

    ready = [both_batches(value) for value in outputs]

    def reduced(value):
        return lax.psum_scatter(value, GROUP, scatter_dimension=0, tiled=True)

    wide_sums = [None, None]
    last_sums = [None, None]
    for layer in (1, 0):
        (
            layer_in,
            joint,
            out_weight,
            up_weight,
            down_weight,
            gain_one,
            gain_two,
            pairs,
            queries,
            mixed,
            lse,
            attended,
            unit_one,
            inverse_one,
            middle_low,
            slope,
            active,
            unit_two,
            inverse_two,
        ) = layers[layer]
        grad_second, grad_gain_two, grad_shift_two = norm_backward(
            grad_top, unit_two, inverse_two, gain_two
        )
        grad_down_low = grad_second.astype(BF16)
        grad_active = jnp.concatenate(
            [dot(grad_down_low, down_weight[at], NT) for at in range(chunks)], axis=1
        )
        grad_hidden = (grad_active * slope).astype(BF16)
        grad_down = [
            dot(active[:, at * width : (at + 1) * width], grad_down_low, TN).astype(BF16)
            for at in range(chunks)
        ]
        grad_up = dot(middle_low, grad_hidden, TN).astype(BF16)
        parts = [grad_up] + grad_down
        wide = jnp.concatenate(parts, axis=1)
        if layer == 0:
            grad_hidden, wide, wide_sums[1] = tied(grad_hidden, wide, wide_sums[1])
        else:
            grad_hidden, wide = tied(grad_hidden, wide)
        wide_sums[layer] = reduced(wide)
        grad_middle = grad_second + dot(grad_hidden, up_weight, NT)
        grad_first, grad_gain_one, grad_shift_one = norm_backward(
            grad_middle, unit_one, inverse_one, gain_one
        )
        grad_branch = grad_first.astype(BF16)
        grad_returned = dot(grad_branch, out_weight, NT).astype(BF16)
        grad_mixed = to_heads(columns(grad_returned, part_width))
        if direct and layer == 0:
            grad_mixed, *last_chip = tied(grad_mixed, *last_chip)
            last_side = side_sum(last_chip)[0]
        grad_queries, grad_pairs = attention_backward(
            queries, pairs, query_ids, key_marks, mixed, lse, grad_mixed
        )
        if direct and layer == 0:
            grad_queries, grad_pairs, last_side = tied(grad_queries, grad_pairs, last_side)
        grad_arrived = jnp.concatenate([own_keys_sum(grad_pairs), grad_queries], axis=1)
        grad_joint = jnp.concatenate(to_tokens(grad_arrived), axis=1)
        grad_input = grad_first + dot(grad_joint, joint, NT)
        joint_sum = jnp.sum(grad_joint.astype(F32), axis=0).reshape(members, 3, part_width)
        small = jnp.stack(
            [
                joint_sum[:, 2].reshape(width),
                joint_sum[:, 1].reshape(width),
                jnp.sum(grad_branch.astype(F32), axis=0),
                grad_gain_one,
                grad_shift_one,
                jnp.sum(grad_down_low.astype(F32), axis=0),
                grad_gain_two,
                grad_shift_two,
            ],
            axis=0,
        )
        hidden_sum = jnp.sum(grad_hidden.astype(F32), axis=0).reshape(chunks, width)
        small = jnp.concatenate([small, hidden_sum], axis=0).astype(BF16)
        small = jnp.pad(small.T, ((0, 0), (0, 128 - small_count)))
        if direct:
            last_chip = chip_parts(
                [
                    jnp.concatenate(group, axis=1)
                    for group in zip(
                        weight_grad(layer_in, grad_joint),
                        weight_grad(attended, grad_branch),
                        halves(small, 0),
                    )
                ]
            )
        else:
            last_sums[layer] = reduced(
                jnp.concatenate(
                    [
                        dot(layer_in, grad_joint, TN).astype(BF16),
                        dot(attended, grad_branch, TN).astype(BF16),
                        small,
                    ],
                    axis=1,
                )
            )
        ready.append(both_batches(grad_input))
        grad_top = grad_input.astype(BF16).astype(F32)

    def settle(first, second):
        to_first = lax.ppermute(first, "section", [(1, 0)])
        to_second = lax.ppermute(second, "section", [(0, 1)])
        return jnp.where(first_section, first, second).astype(F32) + jnp.where(
            first_section, to_first, to_second
        ).astype(F32)

    if direct:
        last_sides = jnp.concatenate([side_sum(last_chip)[0], last_side], axis=-1)
        last_sides, wide_sums[0], *ready[:3] = tied(last_sides, wide_sums[0], *ready[:3])
        both = line_sum(last_sides)
        last_sums = [both[:, : both.shape[1] // 2], both[:, both.shape[1] // 2 :]]
    wide = settle(wide_sums[0], wide_sums[1])
    last_other = across_section(jnp.where(first_section, last_sums[1], last_sums[0]))
    last = jnp.where(first_section, last_sums[0], last_sums[1]).astype(F32) + last_other.astype(F32)
    grad_up = (
        wide[:, :hidden_width]
        .reshape(shard, chunks, head_count * blk_count, shard)
        .transpose(0, 2, 1, 3)
        .reshape(shard, hidden_width)
    )
    grad_down = jnp.concatenate(
        [
            wide[:, hidden_width + at * width : hidden_width + (at + 1) * width]
            for at in range(chunks)
        ],
        axis=0,
    )
    grad_joint = last[:, :joint_width].reshape(shard, members, 3, part_width)
    grad_key, grad_value, grad_query = [
        grad_joint[:, :, at].reshape(shard, width) for at in range(3)
    ]
    grad_out = last[:, 3 * width : 4 * width]
    small = last[:, 4 * width :].T

    outputs_all = placed(ready[0], ready[1])
    grad_inputs = placed(ready[3], ready[2])
    return (
        outputs_all[None],
        grad_inputs[None],
        grad_query[None],
        grad_key[None],
        grad_value[None],
        grad_out[None],
        small[0][None],
        small[1][None],
        small[2][None],
        small[3][None],
        small[4][None],
        grad_up[None],
        small[8 : 8 + chunks].reshape(1, chunks * shard),
        grad_down[None],
        small[5][None],
        small[6][None],
        small[7][None],
    )


def solution(mesh):
    rows = P(None, GROUP, None)
    marks = P(None, GROUP)
    matrix = P("section", GROUP, None)
    vector = P("section", GROUP)
    result = P("section", None, GROUP, None)
    return jax.shard_map(
        body,
        mesh=mesh,
        in_specs=(rows, rows, marks, marks)
        + (matrix,) * 4
        + (vector,) * 5
        + (matrix, vector, matrix, vector, vector, vector),
        out_specs=(result, result)
        + (matrix,) * 4
        + (vector,) * 5
        + (matrix, vector, matrix, vector, vector, vector),
        check_vma=False,
    )
```
